32 devices in a mesh: mp: 2 (over core), gx: 4 (over z), gy: 4 (over y, x).
Axes of the slice: x: 2, y: 2, z: 4, core: 2. Of those that a mesh axis runs over, the one named last changes fastest.
Arguments:
- states: float32 [2, 64, 512, 512], P('mp', None, 'gx', 'gy'), may hold values from -6 to 6
- surface: float32 [2, 8, 512, 512], P('mp', None, 'gx', 'gy'), may hold values from -6 to 6
- land_mask: int32 [512, 512], P('gx', 'gy'), may hold values 0 or 1
- tile_weights: bfloat16 [2, 4, 4, 64, 128, 128], P('mp', 'gx', 'gy'), may hold values from -0.5 to 0.5
- tile_source: int32 [2, 4, 4, 64], P('mp', 'gx', 'gy'), may hold values from 0 to 127
- tile_target: int32 [2, 4, 4, 64, 1], P('mp', 'gx', 'gy'), may hold values from 0 to 15; in each aligned block of 64 rows (0 to 63, 64 to 127, ..., all dimensions but the last counted through in order) at most 8 rows name the same one
- tile_row: int32 [2, 4, 4, 64], P('mp', 'gx', 'gy'), may hold values from 0 to 127
Outputs:
- new_states: float32 [2, 64, 512, 512], P('mp', None, 'gx', 'gy')
- remapped: float32 [2, 8, 512, 512], P('mp', None, 'gx', 'gy')
The draws below stay inside these ranges and needn't reach their ends.
Inputs may be any that keep to these rules, and one draw needn't show every extreme that they name: `tile_target`: among the tiles of one device, no destination device is named by more than 8 tiles, and some device is named by exactly 8.
All inputs are finite; a program needn't handle non-finite values. No bound on the sum of `land_mask` on one device may be relied on, other than what follows from the above.
Results may differ from the reference program's by a relative error of at most 0.0029.
Values sent between devices are 32-bit elements; how exact they have to be, the bound alone decides.
No kernel may reach another device: no remote copies, remote signals or barrier semaphores. Data moves between devices by JAX's collectives and lax.ppermute only.
A program may use at most 192 MiB of HBM per device.

```python
import math
import jax
import jax.numpy as jnp
import numpy as np
from jax import lax

CX = 128
CY = 128
LEV = 64
KF = 8
CAP = 8
TILES = 64
NX = 512
NY = 512
N_GX = 4
N_GY = 4


def set_ends(entries, rng, low, top_value):
    shape = entries.shape
    place = [jax.random.randint(jax.random.fold_in(rng, axis), (), 0, shape[axis]) for axis in range(len(shape))]
    entries = entries.at[tuple(place)].set(low)
    longest = shape.index(max(shape))
    place[longest] = (place[longest] + 1) % shape[longest]
    return entries.at[tuple(place)].set(top_value)


def block_levels(rng, dims, pieces, low, high):
    def one(dim, blocks):
        heights = jax.random.uniform(jax.random.fold_in(jax.random.fold_in(rng, 6), dim), (blocks,), jnp.float32, low / len(pieces), high / len(pieces))
        return jnp.repeat(jnp.exp(heights), dims[dim] // blocks).reshape((-1,) + (1,) * (len(dims) - dim - 1))

    loudness = one(*pieces[0])
    for cut in pieces[1:]:
        loudness = loudness * one(*cut)
    return loudness


def shared_out(rng, own, number, rows, number_of, top, limit, skew):
    sequence = jax.random.permutation(rng, number_of)
    packed, common = shares(number_of, rows * top, limit, skew, True), shares(number_of, rows * top, limit, skew, False)
    places = jnp.arange(number_of)

    def named(sizes, offset_by):
        used = int((sizes > 0).sum())
        fixed = max(1, used // 4)
        passed = fixed + (places - fixed + offset_by * (used - fixed)) % max(1, number_of - fixed)
        return jnp.zeros((number_of,), jnp.int32).at[sequence[jnp.where(places < fixed, places, passed)]].set(jnp.asarray(sizes, jnp.int32))

    sizes = jnp.where(number % 4 == 0, named(packed, number // 4), named(common, number - number // 4 - 1))
    mixed = jax.random.permutation(jax.random.fold_in(own, 3), number_of)
    giver, sink = mixed[0:number_of // 2 * 2:2], mixed[1:number_of // 2 * 2:2]
    room = jnp.minimum(sizes[giver] - 1, limit - sizes[sink]) // 2
    room = jnp.where((giver == sequence[0]) | (sink == sequence[0]) | (sizes[sink] == 0), 0, jnp.maximum(room, 0))
    passed = jax.random.randint(jax.random.fold_in(own, 4), (number_of // 2,), 0, 1 << 20) % (room + 1)
    sizes = sizes.at[giver].add(-passed).at[sink].add(passed)
    labels = jnp.searchsorted(jnp.cumsum(sizes), jnp.arange(rows * top), side="right").astype(jnp.int32)
    listing = labels.reshape(top, rows).T
    listing = listing[jax.random.permutation(jax.random.fold_in(own, 1), rows)]
    offset_by = jax.random.randint(jax.random.fold_in(own, 2), (rows, 1), 0, top)
    return jnp.take_along_axis(listing, (jnp.arange(top)[None, :] + offset_by) % top, axis=1)


def shares(number_of, total, most, skew, full):
    weights = [(1 << 20) // math.isqrt(rank ** skew) + 1 for rank in range(1, number_of + 1)]
    largest = most if full else min(most, max(-(-total // number_of), total * weights[0] // sum(weights)))
    least = 1 if total - largest >= number_of - 1 else 0
    counts, spare = [largest] + [least] * (number_of - 1), total - largest - least * (number_of - 1)
    while spare > 0:
        candidates = [i for i in range(1, number_of) if counts[i] < largest] or [i for i in range(1, number_of) if counts[i] < most]
        mass, remaining = sum([weights[i] for i in candidates]), spare
        for i in candidates:
            addition = min(most - counts[i], max(1, remaining * weights[i] // mass), spare)
            counts[i] = counts[i] + addition
            spare = spare - addition
    return np.array(counts)


def bell_draw(rng, extent, width, reach, pieces=(), held_as=jnp.bfloat16):
    result = width * jax.random.normal(rng, extent, jnp.float32)
    if pieces:
        result = result * block_levels(rng, extent, pieces, -0.22, 0.18)
    return jnp.clip(result, -reach, reach).astype(held_as)


def setup_inputs(seed: int = 0) -> dict:
    key_of = jax.random.split(jax.random.key(seed), 8)
    states = bell_draw(key_of[0], (2, LEV, NX, NY), 1.0, 6.0, ((0, 2), (2, 4), (3, 4)), jnp.float32)
    surface = bell_draw(key_of[1], (2, KF, NX, NY), 1.0, 6.0, ((0, 2), (2, 4), (3, 4)), jnp.float32)
    land_mask = set_ends((jax.random.randint(key_of[2], (NX, NY), 0, 10) < 7).astype(jnp.int32), jax.random.fold_in(key_of[2], 1), 0, 1)
    tile_weights = bell_draw(key_of[3], (2, N_GX, N_GY, TILES, CY, CY), CY ** -0.5, 0.5, ((0, 2), (1, 4), (2, 4)))
    tile_source = set_ends(jax.random.randint(key_of[4], (2, N_GX, N_GY, TILES), 0, CX), jax.random.fold_in(key_of[4], 1), 0, CX - 1).astype(jnp.int32)
    tile_target_keys = jax.random.split(jax.random.fold_in(key_of[5], 1), 2 * N_GX * N_GY * TILES // TILES)
    tile_target_turns = jax.random.permutation(jax.random.fold_in(key_of[5], 3), 2 * N_GX * N_GY * TILES // TILES)
    tile_target = jax.vmap(lambda own, number: shared_out(jax.random.fold_in(key_of[5], 2), own, number, TILES, N_GX * N_GY, 1, CAP, 2))(tile_target_keys, tile_target_turns).reshape((2, N_GX, N_GY, TILES, 1))
    tile_row = set_ends(jax.random.randint(key_of[6], (2, N_GX, N_GY, TILES), 0, CX), jax.random.fold_in(key_of[6], 1), 0, CX - 1).astype(jnp.int32)
    return dict(states=states, surface=surface, land_mask=land_mask, tile_weights=tile_weights, tile_source=tile_source, tile_target=tile_target, tile_row=tile_row)


coef_horiz = (0.15, 0.12)
coef_vert = (0.1, 0.15)
force_gain = 0.5


def stencil(state, wet, horiz, vert):
    weighted = state * wet
    padded = jnp.pad(weighted, ((0, 0), (1, 1), (1, 1)))
    lateral = padded[:, 2:, 1:-1] + padded[:, :-2, 1:-1] + padded[:, 1:-1, 2:] + padded[:, 1:-1, :-2] - 4.0 * weighted
    column = jnp.pad(state, ((1, 1), (0, 0), (0, 0)))
    vertical = column[2:] + column[:-2] - 2.0 * state
    return wet * (state + horiz * lateral + vert * vertical)


def remap_group(surf, wet, weights, source, target, row):
    ndev = N_GX * N_GY
    src = (surf * wet).astype(jnp.bfloat16)
    blocks = src.reshape(KF, N_GX, CX, N_GY, CY).transpose(1, 3, 0, 2, 4).reshape(ndev, KF, CX, CY)

    def one_device(items):
        block, tiles, rows_idx = items
        picked = jnp.take(block, rows_idx, axis=1)
        return jnp.einsum("tji,kti->tkj", tiles.astype(jnp.float32), picked.astype(jnp.float32))

    contrib = lax.map(one_device, (blocks, weights.reshape(ndev, TILES, CY, CY), source.reshape(ndev, TILES).astype(jnp.int32)))
    index = (target.reshape(ndev * TILES) * CX + row.reshape(ndev * TILES)).astype(jnp.int32)
    total = jnp.zeros((ndev * CX, KF, CY), jnp.float32).at[index].add(contrib.reshape(ndev * TILES, KF, CY))
    return total.reshape(N_GX, N_GY, CX, KF, CY).transpose(3, 0, 2, 1, 4).reshape(KF, N_GX * CX, N_GY * CY)


def reference(states, surface, land_mask, tile_weights, tile_source, tile_target, tile_row):
    wets = (jnp.ones((N_GX * CX, N_GY * CY), jnp.float32), land_mask.astype(jnp.float32))
    to_ocean = remap_group(surface[0], wets[0], tile_weights[0], tile_source[0], tile_target[0], tile_row[0])
    to_atmos = remap_group(surface[1], wets[1], tile_weights[1], tile_source[1], tile_target[1], tile_row[1])
    remapped = jnp.stack([to_atmos, to_ocean])
    outputs = []
    for group in range(2):
        first = stencil(states[group], wets[group], coef_horiz[group], coef_vert[group])
        second = stencil(first, wets[group], coef_horiz[group], coef_vert[group])
        second = second.at[0].add(force_gain * wets[group] * remapped[group, 0])
        outputs.append(second)
    return jnp.stack(outputs), remapped
```

```python
import functools

import jax
import jax.numpy as jnp
from jax import lax
from jax.experimental import pallas as pl
from jax.experimental.pallas import tpu as pltpu
from jax.sharding import PartitionSpec as P

CAP = 8
FORCE = 0.5
HORIZ = (0.15, 0.12)
VERT = (0.1, 0.15)
MIB = 1024 * 1024
ANY = pl.BlockSpec(memory_space=pl.ANY)
VMEM = pl.BlockSpec(memory_space=pltpu.VMEM)
SMEM = pl.BlockSpec(memory_space=pltpu.SMEM)


def params(mib):
    return pltpu.CompilerParams(vmem_limit_bytes=mib * MIB)


def wet_of(mask_ref):
    ocean = lax.axis_index("mp") == 1
    return jnp.where(ocean, mask_ref[...].astype(jnp.float32), 1.0)


def lanes(shape):
    return lax.broadcasted_iota(jnp.int32, shape, len(shape) - 1)


def tiles_kernel(ndev, ngy, chunk, src, tgt, row, mask, surface, weights, out, wet, wbuf, sbuf, count, sems):
    tiles = src.shape[0]
    cx = mask.shape[0]
    pieces = tiles // chunk
    copies = [pltpu.make_async_copy(surface, sbuf, sems.at[pieces])]
    for i in range(pieces):
        part = pl.ds(i * chunk, chunk)
        copies.append(pltpu.make_async_copy(weights.at[part], wbuf.at[part], sems.at[i]))
    for copy in copies:
        copy.start()
    wet[...] = wet_of(mask)
    out[...] = jnp.zeros_like(out)
    for d in range(ndev):
        count[d] = 0
    me = lax.axis_index("gx") * ngy + lax.axis_index("gy")
    place = lax.broadcasted_iota(jnp.int32, (8, 128), 0) * 128 + lanes((8, 128))
    copies[0].wait()

    def one(t, _):
        s, d = src[t], tgt[t, 0]
        rank = count[d]
        count[d] = rank + 1
        picked = sbuf[pl.ds(s, 8, stride=cx), :] * wet[pl.ds(s, 1), :]
        out[d, pl.ds(rank * 8, 8), :] = lax.dot_general(
            picked.astype(jnp.bfloat16),
            wbuf[t],
            (((1,), (1,)), ((), ())),
            preferred_element_type=jnp.float32,
        )
        label = (row[t] + 1).astype(jnp.float32)
        out[d, 64:72, :] = jnp.where(place == me * CAP + rank, label, out[d, 64:72, :])
        return 0

    for i in range(pieces):
        copies[i + 1].wait()
        lax.fori_loop(i * chunk, (i + 1) * chunk, one, 0, unroll=True)


def remap_tiles(src, tgt, row, mask, surface, weights, ndev, ngy):
    tiles = src.shape[0]
    chunk = 16
    return pl.pallas_call(
        functools.partial(tiles_kernel, ndev, ngy, chunk),
        out_shape=jax.ShapeDtypeStruct((ndev, 72, 128), jnp.float32),
        in_specs=[SMEM, SMEM, SMEM, VMEM, ANY, ANY],
        out_specs=VMEM,
        scratch_shapes=[
            pltpu.VMEM(mask.shape, jnp.float32),
            pltpu.VMEM(weights.shape, weights.dtype),
            pltpu.VMEM(surface.shape, jnp.float32),
            pltpu.SMEM((ndev,), jnp.int32),
            pltpu.SemaphoreType.DMA((tiles // chunk + 1,)),
        ],
        compiler_params=params(32),
        cost_estimate=pl.CostEstimate(flops=4 * 10**8, bytes_accessed=4 * 10**6, transcendentals=0),
    )(src, tgt, row, mask, surface, weights)


def pack_kernel(group, mask, state, up, down, left, right, wet, buf, sems):
    lev, cx, cy = state.shape
    copies = []
    for i in range(lev // group):
        part = pl.ds(i * group, group)
        copies.append(pltpu.make_async_copy(state.at[part], buf.at[part], sems.at[i]))
        copies[-1].start()
    wet[...] = wet_of(mask)
    turned = jnp.transpose(wet[...])
    up[2 * lev :, :] = jnp.broadcast_to(wet[0:1, :], (8, cy))
    down[2 * lev :, :] = jnp.broadcast_to(wet[cx - 1 :, :], (8, cy))
    left[cx:, :] = jnp.broadcast_to(turned[0:1, :], (8, cx))
    right[cx:, :] = jnp.broadcast_to(turned[cy - 1 :, :], (8, cx))
    strip = 32
    flat = buf.reshape(lev * cx, cy)
    lane = lanes((strip, cy))
    for i in range(lev // group):
        copies[i].wait()
        part = pl.ds(i * group, group)
        for dst, off, r in ((up, 0, 0), (up, lev, 1), (down, 0, cx - 1), (down, lev, cx - 2)):
            dst[pl.ds(off + i * group, group), :] = (
                flat[pl.ds(i * group * cx + r, group, stride=cx), :] * wet[r : r + 1, :]
            )
        for b in range(cx // strip):
            rows = pl.ds(b * strip, strip)
            if i == 0:
                lo = hi = jnp.zeros((strip, cy), jnp.float32)
            else:
                lo, hi = left[rows, :], right[rows, :]
            for l in range(i * group, (i + 1) * group):
                moved = pltpu.roll(buf[l, rows, :], (2 * l + 2) % cy, 1)
                at = (2 * l + 2) % cy
                lo = jnp.where((lane == at) | (lane == at + 1), moved, lo)
                hi = jnp.where((lane == 2 * l) | (lane == 2 * l + 1), moved, hi)
            if i == lev // group - 1:
                edge = wet[rows, :]
                first, second = edge[:, 0:1], edge[:, 1:2]
                lo = lo * jnp.where(lane % 2 == 0, first, second)
                first, second = edge[:, cy - 2 : cy - 1], edge[:, cy - 1 :]
                hi = hi * jnp.where(lane % 2 == 0, first, second)
            left[rows, :] = lo
            right[rows, :] = hi


def pack_edges(mask, state):
    lev, cx, cy = state.shape
    group = 8
    message = jax.ShapeDtypeStruct((2 * lev + 8, cy), jnp.float32)
    columns = jax.ShapeDtypeStruct((cx + 8, cy), jnp.float32)
    return pl.pallas_call(
        functools.partial(pack_kernel, group),
        out_shape=(message, message, columns, columns),
        in_specs=[VMEM, ANY],
        out_specs=(VMEM,) * 4,
        scratch_shapes=[
            pltpu.VMEM(mask.shape, jnp.float32),
            pltpu.VMEM(state.shape, jnp.float32),
            pltpu.SemaphoreType.DMA((lev // group,)),
        ],
        compiler_params=params(16),
        cost_estimate=pl.CostEstimate(flops=10**7, bytes_accessed=4 * 10**6, transcendentals=0),
    )(mask, state)


def shifted(x, by, axis):
    size = x.shape[axis]
    moved = pltpu.roll(x, by % size, axis)
    index = lax.broadcasted_iota(jnp.int32, x.shape, axis)
    return jnp.where(index == (0 if by == 1 else size - 1), 0.0, moved)


PAD = 8


def stencil_kernel(
    group, ngx, ngy, mask, state, up, down, left, right, top, bottom, west, east, cwest, ceast,
    out, wet, hwet, one, two, cols, cols2, res, sems, osems,
):
    lev, cx, cy = state.shape
    pieces = lev // group
    copies = []
    for i in range(pieces):
        part = pl.ds(i * group, group)
        copies.append(
            pltpu.make_async_copy(
                state.at[part], one.at[pl.ds(i * group + 1, group), pl.ds(PAD, cx), :], sems.at[i]
            )
        )
        copies[-1].start()
    ocean = lax.axis_index("mp") == 1
    horiz = jnp.where(ocean, HORIZ[1], HORIZ[0]).astype(jnp.float32)
    vert = jnp.where(ocean, VERT[1], VERT[0]).astype(jnp.float32)
    centre = 1.0 - 4.0 * horiz - 2.0 * vert
    gx, gy = lax.axis_index("gx"), lax.axis_index("gy")
    has = lambda c: jnp.where(c, 1.0, 0.0).astype(jnp.float32)
    has_top, has_bottom = has(gx > 0), has(gx < ngx - 1)
    has_west, has_east = has(gy > 0), has(gy < ngy - 1)
    wet[...] = wet_of(mask)
    hwet[...] = wet[...] * horiz

    lane = lanes((lev, cy))
    flat_one = one.reshape((lev + 2) * (cx + 2 * PAD), cy)
    flat_two = two.reshape((lev + 2) * (cx + 2 * PAD), cy)
    height = cx + 2 * PAD
    for msg, own, flag, off, at in ((top, up, has_top, 0, PAD - 1), (bottom, down, has_bottom, lev, PAD + cx)):
        near = msg[0:lev, :] * flag
        far = msg[lev : 2 * lev, :] * flag
        w_corner = cwest[off : off + lev, :] * (flag * has_west)
        e_corner = ceast[off : off + lev, :] * (flag * has_east)
        side = pltpu.roll(jnp.where(lane == cy - 1, w_corner, near), 1, 1) + pltpu.roll(
            jnp.where(lane == 0, e_corner, near), cy - 1, 1
        )
        gain = msg[2 * lev : 2 * lev + 1, :] * (horiz * flag)
        ring = (
            centre * near
            + gain * (side + far + own[0:lev, :])
            + vert * (shifted(near, 1, 0) + shifted(near, -1, 0))
        )
        flat_one[pl.ds(height + at, lev, stride=height), :] = near
        flat_two[pl.ds(height + at, lev, stride=height), :] = ring

    lane = lanes((cx, cy))
    odd = lane % 2 == 1
    west_cols = west[0:cx, :] * has_west
    east_cols = east[0:cx, :] * has_east
    w_gain = jnp.transpose(jnp.broadcast_to(west[cx : cx + 1, :], (cx, cx))) * (horiz * has_west)
    e_gain = jnp.transpose(jnp.broadcast_to(east[cx : cx + 1, :], (cx, cx))) * (horiz * has_east)
    merged = jnp.where(odd, west_cols, east_cols)
    cols[...] = merged
    beside = (
        jnp.where(odd, pltpu.roll(west_cols, 1, 1), pltpu.roll(east_cols, cy - 1, 1))
        + jnp.where(odd, pltpu.roll(left[0:cx, :], cy - 1, 1), pltpu.roll(right[0:cx, :], 1, 1))
    )
    eye = lanes((lev, cy)) - 2 * lax.broadcasted_iota(jnp.int32, (lev, cy), 0)
    eye_w = eye == 1
    eye_e = (eye == 2) | (eye == 2 - cy)

    def corner_row(off, flag):
        w = cwest[off : off + lev, cy - 1 : cy] * (flag * has_west)
        e = ceast[off : off + lev, 0:1] * (flag * has_east)
        return jnp.sum(jnp.where(eye_w, w, 0.0) + jnp.where(eye_e, e, 0.0), axis=0, keepdims=True)

    sub = lax.broadcasted_iota(jnp.int32, (cx, cy), 0)
    above = jnp.where(sub == 0, corner_row(0, has_top), pltpu.roll(merged, 1, 0))
    below = jnp.where(sub == cx - 1, corner_row(lev, has_bottom), pltpu.roll(merged, cx - 1, 0))
    less = jnp.where((lane == 1) | (lane == 2), 0.0, pltpu.roll(merged, 2, 1))
    more = jnp.where((lane == cy - 1) | (lane == 0), 0.0, pltpu.roll(merged, cy - 2, 1))
    cols2[...] = (
        centre * merged
        + jnp.where(odd, w_gain, e_gain) * (beside + above + below)
        + vert * (less + more)
    )

    for buf in (one, two):
        buf[0] = jnp.zeros((height, cy), jnp.float32)
        buf[lev + 1] = jnp.zeros((height, cy), jnp.float32)

    strip = 64

    def mask_level(l, _):
        one[l + 1, PAD : PAD + cx, :] = one[l + 1, PAD : PAD + cx, :] * wet[...]
        return 0

    def step(buf, sides, l, b):
        lane = lanes((strip, cy))
        r = PAD + b * strip
        here = buf[l + 1, r : r + strip, :]
        edge = pltpu.roll(sides[b * strip : (b + 1) * strip, :], (2 * cy - 2 * l - 2) % cy, 1)
        around = (
            pltpu.roll(jnp.where(lane == cy - 1, edge, here), 1, 1)
            + pltpu.roll(jnp.where(lane == 0, edge, here), cy - 1, 1)
            + buf[l + 1, r - 1 : r - 1 + strip, :]
            + buf[l + 1, r + 1 : r + 1 + strip, :]
        )
        column = buf[l, r : r + strip, :] + buf[l + 2, r : r + strip, :]
        return centre * here + hwet[b * strip : (b + 1) * strip, :] * around + vert * column

    def first_level(l, _):
        for b in range(cx // strip):
            two[l + 1, PAD + b * strip : PAD + (b + 1) * strip, :] = step(one, cols, l, b)
        return 0

    def second_level(l, _):
        for b in range(cx // strip):
            res[l, b * strip : (b + 1) * strip, :] = step(two, cols2, l, b)
        return 0

    outs = []
    for i in range(pieces + 2):
        if i < pieces:
            copies[i].wait()
            lax.fori_loop(i * group, (i + 1) * group, mask_level, 0, unroll=2)
        a, b = max(0, i * group - 1), min(lev, (i + 1) * group - 1)
        if i >= pieces:
            a, b = max(a, lev - 1), lev
        if i <= pieces and a < b:
            lax.fori_loop(a, b, first_level, 0, unroll=False)
        if i >= 1 and i <= pieces:
            start, stop = (i - 1) * group, i * group
            lax.fori_loop(start, stop, second_level, 0, unroll=False)
            part = pl.ds(start, group)
            outs.append(pltpu.make_async_copy(res.at[part], out.at[part], osems.at[i - 1]))
            outs[-1].start()
    for copy in outs:
        copy.wait()


def two_steps(mask, state, messages, ngx, ngy):
    lev, cx, cy = state.shape
    group = 8
    padded = (lev + 2, cx + 2 * PAD, cy)
    return pl.pallas_call(
        functools.partial(stencil_kernel, group, ngx, ngy),
        out_shape=jax.ShapeDtypeStruct(state.shape, jnp.float32),
        in_specs=[VMEM, ANY] + [VMEM] * len(messages),
        out_specs=ANY,
        scratch_shapes=[
            pltpu.VMEM((cx, cy), jnp.float32),
            pltpu.VMEM((cx, cy), jnp.float32),
            pltpu.VMEM(padded, jnp.float32),
            pltpu.VMEM(padded, jnp.float32),
            pltpu.VMEM((cx, cy), jnp.float32),
            pltpu.VMEM((cx, cy), jnp.float32),
            pltpu.VMEM(state.shape, jnp.float32),
            pltpu.SemaphoreType.DMA((lev // group,)),
            pltpu.SemaphoreType.DMA((lev // group,)),
        ],
        compiler_params=params(40),
        cost_estimate=pl.CostEstimate(flops=2 * 10**7, bytes_accessed=10**7, transcendentals=0),
    )(mask, state, *messages)


def collect_kernel(mask, got, second, out, received, buf, level, onehot, sems):
    ndev = got.shape[0]
    fields, cx, cy = received.shape
    slots = ndev * CAP
    fetch = pltpu.make_async_copy(got, buf, sems.at[0])
    fetch.start()
    surface = pltpu.make_async_copy(second.at[0], level, sems.at[1])
    surface.start()
    fetch.wait()
    flat = buf.reshape(ndev * 72, 128)
    labels = flat[64:72, :]
    for s in range(1, ndev):
        labels = labels + flat[s * 72 + 64 : s * 72 + 72, :]
    labels = labels.astype(jnp.int32)
    want = lax.broadcasted_iota(jnp.int32, (cx, 128), 0) + 1
    wide = jnp.concatenate([labels[q : q + 1, :] == want for q in range(slots // 128)], axis=1)
    hot = jnp.where(wide, 1.0, 0.0).astype(jnp.bfloat16)
    onehot[:, 0:slots] = hot
    onehot[:, slots:] = hot
    surface.wait()
    for k in range(fields):
        x = jnp.concatenate([flat[pl.ds(s * 72 + k, CAP, stride=8), :] for s in range(ndev)], axis=0)
        high = x.astype(jnp.bfloat16)
        low = (x - high.astype(jnp.float32)).astype(jnp.bfloat16)
        total = jnp.dot(
            onehot[...], jnp.concatenate([high, low], axis=0), preferred_element_type=jnp.float32
        )
        received[k] = total
        if k == 0:
            level[...] = level[...] + FORCE * wet_of(mask) * total
            store = pltpu.make_async_copy(level, out.at[0], sems.at[1])
            store.start()
    store.wait()


def collect(mask, got, second, fields):
    ndev = got.shape[0]
    cx, cy = mask.shape
    return pl.pallas_call(
        collect_kernel,
        out_shape=(
            jax.ShapeDtypeStruct(second.shape, jnp.float32),
            jax.ShapeDtypeStruct((fields, cx, cy), jnp.float32),
        ),
        in_specs=[VMEM, ANY, ANY],
        out_specs=(ANY, VMEM),
        scratch_shapes=[
            pltpu.VMEM(got.shape, jnp.float32),
            pltpu.VMEM((cx, cy), jnp.float32),
            pltpu.VMEM((cx, 2 * ndev * CAP), jnp.bfloat16),
            pltpu.SemaphoreType.DMA((2,)),
        ],
        input_output_aliases={2: 0},
        compiler_params=params(16),
        cost_estimate=pl.CostEstimate(flops=10**8, bytes_accessed=2 * 10**6, transcendentals=0),
    )(mask, got, second)


def local(states, surface, land_mask, tile_weights, tile_source, tile_target, tile_row):
    ngx, ngy = lax.axis_size("gx"), lax.axis_size("gy")
    ndev = ngx * ngy
    state, fields = states[0], surface.shape[1]
    cx, cy = land_mask.shape
    buckets = remap_tiles(
        tile_source[0, 0, 0],
        tile_target[0, 0, 0],
        tile_row[0, 0, 0],
        land_mask,
        surface.reshape(fields * cx, cy),
        tile_weights[0, 0, 0],
        ndev,
        ngy,
    )
    buckets = lax.ppermute(buckets, "mp", [(0, 1), (1, 0)])
    got = lax.all_to_all(buckets, ("gx", "gy"), split_axis=0, concat_axis=0, tiled=True)

    ahead = lambda n: [(i, (i + 1) % n) for i in range(n)]
    behind = lambda n: [((i + 1) % n, i) for i in range(n)]
    up, down, left, right = pack_edges(land_mask, state)
    top = lax.ppermute(down, "gx", ahead(ngx))
    bottom = lax.ppermute(up, "gx", behind(ngx))
    west = lax.ppermute(right, "gy", ahead(ngy))
    east = lax.ppermute(left, "gy", behind(ngy))
    lev = state.shape[0]
    rows = jnp.concatenate([top[:lev], bottom[:lev]], axis=0)
    corner_west = lax.ppermute(rows, "gy", ahead(ngy))
    corner_east = lax.ppermute(rows, "gy", behind(ngy))
    messages = (up, down, left, right, top, bottom, west, east, corner_west, corner_east)
    second = two_steps(land_mask, state, messages, ngx, ngy)
    new_state, received = collect(land_mask, got, second, fields)
    return new_state[None], received[None]


def solution(mesh):
    return jax.shard_map(
        local,
        mesh=mesh,
        in_specs=(
            P("mp", None, "gx", "gy"),
            P("mp", None, "gx", "gy"),
            P("gx", "gy"),
            P("mp", "gx", "gy", None, None, None),
            P("mp", "gx", "gy", None),
            P("mp", "gx", "gy", None, None),
            P("mp", "gx", "gy", None),
        ),
        out_specs=(P("mp", None, "gx", "gy"), P("mp", None, "gx", "gy")),
        check_vma=False,
    )
```

```python
import functools

import jax
import jax.numpy as jnp
from jax import lax
from jax.experimental import pallas as pl
from jax.experimental.pallas import tpu as pltpu
from jax.sharding import PartitionSpec as P

CAP = 8
FORCE = 0.5
HORIZ = (0.15, 0.12)
VERT = (0.1, 0.15)
MIB = 1024 * 1024
LIMIT = 60
ANY = pl.BlockSpec(memory_space=pl.ANY)
VMEM = pl.BlockSpec(memory_space=pltpu.VMEM)
SMEM = pl.BlockSpec(memory_space=pltpu.SMEM)


def params(mib):
    return pltpu.CompilerParams(vmem_limit_bytes=mib * MIB)


def wet_of(mask_ref):
    ocean = lax.axis_index("mp") == 1
    return jnp.where(ocean, mask_ref[...].astype(jnp.float32), 1.0)


def lanes(shape):
    return lax.broadcasted_iota(jnp.int32, shape, len(shape) - 1)


def send_kernel(
    ndev, ngy, chunk, group, tile_source, tile_target, tile_row, mask, surface, weights, state,
    out, up, down, left, right, wet,
    src, tgt, row, count, labels, mbuf, sbuf, wbuf, buf, sems, wsems, usems,
):
    lev, cx, cy = state.shape
    tiles = weights.shape[0]
    small = [
        pltpu.make_async_copy(a, b, sems.at[i])
        for i, (a, b) in enumerate(
            ((tile_source, src), (tile_target, tgt), (tile_row, row), (mask, mbuf), (surface, sbuf))
        )
    ]
    for copy in small:
        copy.start()
    wcopies, ucopies = [], []
    for i in range(tiles // chunk):
        part = pl.ds(i * chunk, chunk)
        wcopies.append(pltpu.make_async_copy(weights.at[part], wbuf.at[part], wsems.at[i]))
        wcopies[-1].start()
    for i in range(lev // group):
        part = pl.ds(i * group, group)
        ucopies.append(pltpu.make_async_copy(state.at[part], buf.at[part], usems.at[i]))
        ucopies[-1].start()
    out[...] = jnp.zeros_like(out)
    labels[...] = jnp.zeros_like(labels)
    for d in range(ndev):
        count[d] = 0
    me = lax.axis_index("gx") * ngy + lax.axis_index("gy")
    place = lax.broadcasted_iota(jnp.int32, (8, 128), 0) * 128 + lanes((8, 128))
    for copy in small:
        copy.wait()
    wet[...] = wet_of(mbuf)

    def one(t, _):
        s, d = src[t], tgt[t]
        rank = count[d]
        count[d] = rank + 1
        picked = sbuf[pl.ds(s, 8, stride=cx), :] * wet[pl.ds(s, 1), :]
        out[d, pl.ds(rank * 8, 8), :] = lax.dot_general(
            picked.astype(jnp.bfloat16),
            wbuf[t],
            (((1,), (1,)), ((), ())),
            preferred_element_type=jnp.float32,
        )
        label = (row[t] + 1).astype(jnp.float32)
        labels[d] = jnp.where(place == me * CAP + rank, label, labels[d])
        return 0

    for i in range(tiles // chunk):
        wcopies[i].wait()
        lax.fori_loop(i * chunk, (i + 1) * chunk, one, 0, unroll=True)
    for d in range(ndev):
        out[d, 64:72, :] = labels[d]

    turned = jnp.transpose(wet[...])
    up[2 * lev :, :] = jnp.broadcast_to(wet[0:1, :], (8, cy))
    down[2 * lev :, :] = jnp.broadcast_to(wet[cx - 1 :, :], (8, cy))
    left[cx:, :] = jnp.broadcast_to(turned[0:1, :], (8, cx))
    right[cx:, :] = jnp.broadcast_to(turned[cy - 1 :, :], (8, cx))
    strip = 32
    flat = buf.reshape(lev * cx, cy)
    lane = lanes((strip, cy))
    for i in range(lev // group):
        ucopies[i].wait()
        for dst, off, r in ((up, 0, 0), (up, lev, 1), (down, 0, cx - 1), (down, lev, cx - 2)):
            dst[pl.ds(off + i * group, group), :] = (
                flat[pl.ds(i * group * cx + r, group, stride=cx), :] * wet[r : r + 1, :]
            )
        for b in range(cx // strip):
            rows = pl.ds(b * strip, strip)
            if i == 0:
                lo = hi = jnp.zeros((strip, cy), jnp.float32)
            else:
                lo, hi = left[rows, :], right[rows, :]
            for l in range(i * group, (i + 1) * group):
                moved = pltpu.roll(buf[l, rows, :], (2 * l + 2) % cy, 1)
                at = (2 * l + 2) % cy
                lo = jnp.where((lane == at) | (lane == at + 1), moved, lo)
                hi = jnp.where((lane == 2 * l) | (lane == 2 * l + 1), moved, hi)
            if i == lev // group - 1:
                edge = wet[rows, :]
                first, second = edge[:, 0:1], edge[:, 1:2]
                lo = lo * jnp.where(lane % 2 == 0, first, second)
                first, second = edge[:, cy - 2 : cy - 1], edge[:, cy - 1 :]
                hi = hi * jnp.where(lane % 2 == 0, first, second)
            left[rows, :] = lo
            right[rows, :] = hi


def outgoing(tile_source, tile_target, tile_row, mask, surface, weights, state, ngx, ngy):
    tiles = weights.shape[0]
    lev, cx, cy = state.shape
    ndev, chunk, group = ngx * ngy, 32, 16
    message = jax.ShapeDtypeStruct((2 * lev + 8, cy), jnp.float32)
    columns = jax.ShapeDtypeStruct((cx + 8, cy), jnp.float32)
    return pl.pallas_call(
        functools.partial(send_kernel, ndev, ngy, chunk, group),
        out_shape=(
            jax.ShapeDtypeStruct((ndev, 72, 128), jnp.float32),
            message,
            message,
            columns,
            columns,
            jax.ShapeDtypeStruct(mask.shape, jnp.float32),
        ),
        in_specs=[ANY] * 7,
        out_specs=(VMEM,) * 6,
        scratch_shapes=[
            pltpu.SMEM((tiles,), jnp.int32),
            pltpu.SMEM((tiles,), jnp.int32),
            pltpu.SMEM((tiles,), jnp.int32),
            pltpu.SMEM((ndev,), jnp.int32),
            pltpu.VMEM((ndev, 8, 128), jnp.float32),
            pltpu.VMEM(mask.shape, jnp.int32),
            pltpu.VMEM(surface.shape, jnp.float32),
            pltpu.VMEM(weights.shape, weights.dtype),
            pltpu.VMEM(state.shape, jnp.float32),
            pltpu.SemaphoreType.DMA((5,)),
            pltpu.SemaphoreType.DMA((tiles // chunk,)),
            pltpu.SemaphoreType.DMA((lev // group,)),
        ],
        compiler_params=params(LIMIT),
        cost_estimate=pl.CostEstimate(flops=10**8, bytes_accessed=8 * 10**6, transcendentals=0),
    )(tile_source, tile_target, tile_row, mask, surface, weights, state)


def shifted(x, by, axis):
    size = x.shape[axis]
    moved = pltpu.roll(x, by % size, axis)
    index = lax.broadcasted_iota(jnp.int32, x.shape, axis)
    return jnp.where(index == (0 if by == 1 else size - 1), 0.0, moved)


PAD = 8


def ring_kernel(ngx, ngy, lev, wet, up, down, left, right, east, west, bottom, top, ring, gains, rows):
    cx, cy = wet.shape
    ocean = lax.axis_index("mp") == 1
    horiz = jnp.where(ocean, HORIZ[1], HORIZ[0]).astype(jnp.float32)
    vert = jnp.where(ocean, VERT[1], VERT[0]).astype(jnp.float32)
    centre = 1.0 - 4.0 * horiz - 2.0 * vert
    gx, gy = lax.axis_index("gx"), lax.axis_index("gy")
    has = lambda c: jnp.where(c, 1.0, 0.0).astype(jnp.float32)
    has_top, has_bottom = has(gx > 0), has(gx < ngx - 1)
    has_west, has_east = has(gy > 0), has(gy < ngy - 1)

    lane = lanes((lev, cy))
    edge_lane = lanes((1, cy))
    for msg, own, flag, i in ((top, up, has_top, 0), (bottom, down, has_bottom, 1)):
        rows[i * lev : (i + 1) * lev, :] = msg[0:lev, :]
        near = msg[0:lev, :] * flag
        far = msg[lev : 2 * lev, :] * flag
        side = shifted(near, 1, 1) + shifted(near, -1, 1)
        end = i * (cx - 1)
        beside = jnp.where(
            edge_lane == 0, west[cx : cx + 1, end : end + 1] * has_west, 0.0
        ) + jnp.where(edge_lane == cy - 1, east[cx : cx + 1, end : end + 1] * has_east, 0.0)
        reach = jnp.where(edge_lane == 0, has_west, jnp.where(edge_lane == cy - 1, has_east, 0.0))
        total = (msg[2 * lev : 2 * lev + 1, :] * flag + beside) * (wet[end : end + 1, :] * reach)
        gains[8 * i : 8 * i + 8, :] = jnp.broadcast_to(total * (horiz * horiz * flag), (8, cy))
        gain = msg[2 * lev : 2 * lev + 1, :] * (horiz * flag)
        outer = (
            centre * near
            + gain * (side + far + own[0:lev, :])
            + vert * (shifted(near, 1, 0) + shifted(near, -1, 0))
        )
        ring[2 * i * lev : (2 * i + 1) * lev, :] = near
        ring[(2 * i + 1) * lev : (2 * i + 2) * lev, :] = outer

    lane = lanes((cx, cy))
    odd = lane % 2 == 1
    west_cols = west[0:cx, :] * has_west
    east_cols = east[0:cx, :] * has_east
    w_gain = jnp.transpose(jnp.broadcast_to(west[cx : cx + 1, :], (cx, cx))) * (horiz * has_west)
    e_gain = jnp.transpose(jnp.broadcast_to(east[cx : cx + 1, :], (cx, cx))) * (horiz * has_east)
    merged = jnp.where(odd, west_cols, east_cols)
    ring[4 * lev : 4 * lev + cx, :] = pltpu.roll(jnp.where(odd, merged, pltpu.roll(merged, cy - 2, 1)), cy - 1, 1)
    beside = (
        jnp.where(odd, pltpu.roll(west_cols, 1, 1), pltpu.roll(east_cols, cy - 1, 1))
        + jnp.where(odd, pltpu.roll(left[0:cx, :], cy - 1, 1), pltpu.roll(right[0:cx, :], 1, 1))
    )
    above, below = shifted(merged, 1, 0), shifted(merged, -1, 0)
    less = jnp.where((lane == 1) | (lane == 2), 0.0, pltpu.roll(merged, 2, 1))
    more = jnp.where((lane == cy - 1) | (lane == 0), 0.0, pltpu.roll(merged, cy - 2, 1))
    merged = (
        centre * merged
        + jnp.where(odd, w_gain, e_gain) * (beside + above + below)
        + vert * (less + more)
    )
    ring[4 * lev + cx :, :] = pltpu.roll(jnp.where(odd, merged, pltpu.roll(merged, cy - 2, 1)), cy - 1, 1)


def outer_ring(wet, messages, lev, ngx, ngy):
    cx, cy = wet.shape
    return pl.pallas_call(
        functools.partial(ring_kernel, ngx, ngy, lev),
        out_shape=(
            jax.ShapeDtypeStruct((4 * lev + 2 * cx, cy), jnp.float32),
            jax.ShapeDtypeStruct((16, cy), jnp.float32),
            jax.ShapeDtypeStruct((2 * lev, cy), jnp.float32),
        ),
        in_specs=[VMEM] * 9,
        out_specs=(VMEM, VMEM, VMEM),
        compiler_params=params(LIMIT),
        cost_estimate=pl.CostEstimate(flops=10**11, bytes_accessed=10**8, transcendentals=0),
    )(wet, *messages)


def stencil_kernel(
    group, wet, state, ring, out, hwet, one, two, rbuf, res, sems, osems,
):
    lev, cx, cy = state.shape
    pieces = lev // group
    fetch = pltpu.make_async_copy(ring, rbuf, sems.at[pieces])
    fetch.start()
    copies = []
    for i in range(pieces):
        part = pl.ds(i * group, group)
        copies.append(
            pltpu.make_async_copy(
                state.at[part], one.at[pl.ds(i * group + 1, group), pl.ds(PAD, cx), :], sems.at[i]
            )
        )
        copies[-1].start()
    ocean = lax.axis_index("mp") == 1
    horiz = jnp.where(ocean, HORIZ[1], HORIZ[0]).astype(jnp.float32)
    vert = jnp.where(ocean, VERT[1], VERT[0]).astype(jnp.float32)
    centre = 1.0 - 4.0 * horiz - 2.0 * vert
    hwet[...] = wet[...] * horiz
    lane = lanes((cx, cy))
    height = cx + 2 * PAD
    flat_one = one.reshape((lev + 2) * height, cy)
    flat_two = two.reshape((lev + 2) * height, cy)
    fetch.wait()
    for buf, off, at in (
        (flat_one, 0, PAD - 1),
        (flat_two, lev, PAD - 1),
        (flat_one, 2 * lev, PAD + cx),
        (flat_two, 3 * lev, PAD + cx),
    ):
        buf[pl.ds(height + at, lev, stride=height), :] = rbuf[off : off + lev, :]
    for buf in (one, two):
        buf[0] = jnp.zeros((height, cy), jnp.float32)
        buf[lev + 1] = jnp.zeros((height, cy), jnp.float32)

    def mask_level(l, _):
        one[l + 1, PAD : PAD + cx, :] = one[l + 1, PAD : PAD + cx, :] * wet[...]
        return 0

    ends = (lane == 0) | (lane == cy - 1)
    apart = lax.broadcasted_iota(jnp.int32, (cy, cy), 0) - lanes((cy, cy))
    pairs = jnp.where((apart == 1) | (apart == -1), 1.0, 0.0).astype(jnp.bfloat16)
    pairs = jnp.concatenate([pairs, pairs], axis=0)

    def beside_of(here):
        high = here.astype(jnp.bfloat16)
        low = (here - high.astype(jnp.float32)).astype(jnp.bfloat16)
        both = jnp.concatenate([high, low], axis=1)
        return jnp.dot(both, pairs, preferred_element_type=jnp.float32)

    def step(buf, sides, l, j):
        here = buf[l + 1, PAD : PAD + cx, :]
        edge = pltpu.roll(sides, (cy - 2 * j) % cy, 1)
        around = (
            jnp.where(ends, edge, 0.0)
            + beside_of(here)
            + buf[l + 1, PAD - 1 : PAD - 1 + cx, :]
            + buf[l + 1, PAD + 1 : PAD + 1 + cx, :]
        )
        column = buf[l, PAD : PAD + cx, :] + buf[l + 2, PAD : PAD + cx, :]
        return centre * here + hwet[...] * around + vert * column

    def first_levels(start, count, turn):
        sides = pltpu.roll(rbuf[4 * lev : 4 * lev + cx, :], lax.rem(2 * cy - 2 * start, cy), 1)
        for j in range(count):
            two[start + j + 1, PAD : PAD + cx, :] = step(one, sides, start + j, j)

    def second_levels(start, count):
        sides = pltpu.roll(rbuf[4 * lev + cx :, :], lax.rem(2 * cy - 2 * start, cy), 1)
        for j in range(count):
            res[start + j] = step(two, sides, start + j, j)

    def arrive(i):
        pltpu.make_async_copy(
            state.at[pl.ds(i * group, group)],
            one.at[pl.ds(i * group + 1, group), pl.ds(PAD, cx), :],
            sems.at[i],
        ).wait()
        for j in range(group):
            mask_level(i * group + j, 0)

    def leave(i):
        part = pl.ds(i * group, group)
        return pltpu.make_async_copy(res.at[part], out.at[part], osems.at[i])

    arrive(0)
    first_levels(0, group - 1, 0)

    def middle(i, _):
        arrive(i)
        first_levels(i * group - 1, group, 0)
        second_levels((i - 1) * group, group)
        leave(i - 1).start()
        return 0

    lax.fori_loop(1, pieces, middle, 0)
    first_levels(lev - 1, 1, 0)
    second_levels(lev - group, group)
    leave(pieces - 1).start()
    for i in range(pieces):
        leave(i).wait()


def two_steps(wet, state, ring):
    lev, cx, cy = state.shape
    group = 8
    padded = (lev + 2, cx + 2 * PAD, cy)
    return pl.pallas_call(
        functools.partial(stencil_kernel, group),
        out_shape=jax.ShapeDtypeStruct(state.shape, jnp.float32),
        in_specs=[VMEM, ANY, ANY],
        out_specs=ANY,
        scratch_shapes=[
            pltpu.VMEM((cx, cy), jnp.float32),
            pltpu.VMEM(padded, jnp.float32),
            pltpu.VMEM(padded, jnp.float32),
            pltpu.VMEM(ring.shape, jnp.float32),
            pltpu.VMEM(state.shape, jnp.float32),
            pltpu.SemaphoreType.DMA((lev // group + 1,)),
            pltpu.SemaphoreType.DMA((lev // group,)),
        ],
        compiler_params=params(LIMIT),
        cost_estimate=pl.CostEstimate(flops=10**6, bytes_accessed=10**5, transcendentals=0),
    )(wet, state, ring)


def collect_kernel(
    wet, gains, cwest, ceast, got, second, out, received, level, upper, lower, onehot, sums, sems, rsems
):
    ndev = got.shape[0]
    fields, cx, cy = received.shape
    lev = second.shape[0]
    slots = ndev * CAP

    def move(i, back):
        deep = pl.ds(1, lev - 1)
        here = (level, upper, lower)[i]
        there = (
            lambda r: r.at[0],
            lambda r: r.at[deep, pl.ds(0, 8), :],
            lambda r: r.at[deep, pl.ds(cx - 8, 8), :],
        )[i]
        if back:
            return pltpu.make_async_copy(here, there(out), sems.at[i])
        return pltpu.make_async_copy(there(second), here, sems.at[i])

    def leave(k):
        return pltpu.make_async_copy(sums.at[k], received.at[k], rsems.at[k])

    for i in range(3):
        move(i, False).start()
    flat = got.reshape(ndev * 72, 128)
    labels = flat[64:72, :]
    for s in range(1, ndev):
        labels = labels + flat[s * 72 + 64 : s * 72 + 72, :]
    labels = labels.astype(jnp.int32)
    want = lax.broadcasted_iota(jnp.int32, (cx, 128), 0) + 1
    wide = jnp.concatenate([labels[q : q + 1, :] == want for q in range(slots // 128)], axis=1)
    hot = jnp.where(wide, 1.0, 0.0).astype(jnp.bfloat16)
    onehot[:, 0:slots] = hot
    onehot[:, slots:] = hot
    corners = []
    lane = lanes((lev, cy))
    for i, off in ((0, 0), (1, lev)):
        diagonal = jnp.where(
            lane == 0,
            pltpu.roll(cwest[off : off + lev, :], 1, 1),
            pltpu.roll(ceast[off : off + lev, :], cy - 1, 1),
        )
        corners.append(diagonal * gains[8 * i : 8 * i + 1, :])
    for k in range(fields):
        x = jnp.concatenate([flat[pl.ds(s * 72 + k, CAP, stride=8), :] for s in range(ndev)], axis=0)
        high = x.astype(jnp.bfloat16)
        low = (x - high.astype(jnp.float32)).astype(jnp.bfloat16)
        sums[k] = jnp.dot(
            onehot[...], jnp.concatenate([high, low], axis=0), preferred_element_type=jnp.float32
        )
        leave(k).start()
        if k == 0:
            move(0, False).wait()
            level[...] = level[...] + FORCE * wet[...] * sums[0]
            level[0:1, :] = level[0:1, :] + corners[0][0:1, :]
            level[cx - 1 :, :] = level[cx - 1 :, :] + corners[1][0:1, :]
            move(0, True).start()
            for i, edge, r in ((1, upper, 0), (2, lower, 7)):
                move(i, False).wait()
                rows = edge.reshape((lev - 1) * 8, cy)
                at = pl.ds(r, lev - 1, stride=8)
                rows[at, :] = rows[at, :] + corners[i - 1][1:, :]
                move(i, True).start()
    for i in range(3):
        move(i, True).wait()
    for k in range(fields):
        leave(k).wait()


def collect(wet, gains, corners, got, second, fields):
    ndev = got.shape[0]
    cx, cy = wet.shape
    lev = second.shape[0]
    return pl.pallas_call(
        collect_kernel,
        out_shape=(
            jax.ShapeDtypeStruct(second.shape, jnp.float32),
            jax.ShapeDtypeStruct((fields, cx, cy), jnp.float32),
        ),
        in_specs=[VMEM] * 5 + [ANY],
        out_specs=(ANY, ANY),
        scratch_shapes=[
            pltpu.VMEM((cx, cy), jnp.float32),
            pltpu.VMEM((lev - 1, 8, cy), jnp.float32),
            pltpu.VMEM((lev - 1, 8, cy), jnp.float32),
            pltpu.VMEM((cx, 2 * ndev * CAP), jnp.bfloat16),
            pltpu.VMEM((fields, cx, cy), jnp.float32),
            pltpu.SemaphoreType.DMA((3,)),
            pltpu.SemaphoreType.DMA((fields,)),
        ],
        input_output_aliases={5: 0},
        compiler_params=params(16),
        cost_estimate=pl.CostEstimate(flops=10**8, bytes_accessed=2 * 10**6, transcendentals=0),
    )(wet, gains, *corners, got, second)


def local(states, surface, land_mask, tile_weights, tile_source, tile_target, tile_row):
    ngx, ngy = lax.axis_size("gx"), lax.axis_size("gy")
    ndev = ngx * ngy
    state, fields = states[0], surface.shape[1]
    cx, cy = land_mask.shape
    lev = state.shape[0]
    ahead = lambda n: [(i, (i + 1) % n) for i in range(n)]
    behind = lambda n: [((i + 1) % n, i) for i in range(n)]
    buckets, up, down, left, right, wet = outgoing(
        tile_source[0, 0, 0],
        tile_target[0, 0, 0, :, 0],
        tile_row[0, 0, 0],
        land_mask,
        surface.reshape(fields * cx, cy),
        tile_weights[0, 0, 0],
        state,
        ngx,
        ngy,
    )
    top = lax.ppermute(down, "gx", ahead(ngx))
    bottom = lax.ppermute(up, "gx", behind(ngx))
    west = lax.ppermute(right, "gy", ahead(ngy))
    east = lax.ppermute(left, "gy", behind(ngy))
    buckets = lax.ppermute(buckets, "mp", [(0, 1), (1, 0)])
    got = lax.all_to_all(buckets, ("gx", "gy"), split_axis=0, concat_axis=0, tiled=True)
    messages = (up, down, left, right, east, west, bottom, top)
    ring, gains, rows = outer_ring(wet, messages, lev, ngx, ngy)
    corners = (lax.ppermute(rows, "gy", ahead(ngy)), lax.ppermute(rows, "gy", behind(ngy)))
    second = two_steps(wet, state, ring)
    new_state, received = collect(wet, gains, corners, got, second, fields)
    return new_state[None], received[None]


def solution(mesh):
    return jax.shard_map(
        local,
        mesh=mesh,
        in_specs=(
            P("mp", None, "gx", "gy"),
            P("mp", None, "gx", "gy"),
            P("gx", "gy"),
            P("mp", "gx", "gy", None, None, None),
            P("mp", "gx", "gy", None),
            P("mp", "gx", "gy", None, None),
            P("mp", "gx", "gy", None),
        ),
        out_specs=(P("mp", None, "gx", "gy"), P("mp", None, "gx", "gy")),
        check_vma=False,
    )
```

```python
import functools

import jax
import jax.numpy as jnp
from jax import lax
from jax.experimental import pallas as pl
from jax.experimental.pallas import tpu as pltpu
from jax.sharding import PartitionSpec as P

CAP = 8
FORCE = 0.5
HORIZ = (0.15, 0.12)
VERT = (0.1, 0.15)
MIB = 1024 * 1024
LIMIT = 60
ANY = pl.BlockSpec(memory_space=pl.ANY)
VMEM = pl.BlockSpec(memory_space=pltpu.VMEM)
SMEM = pl.BlockSpec(memory_space=pltpu.SMEM)


def params(mib):
    return pltpu.CompilerParams(vmem_limit_bytes=mib * MIB)


def wet_of(mask_ref):
    ocean = lax.axis_index("mp") == 1
    return jnp.where(ocean, mask_ref[...].astype(jnp.float32), 1.0)


def lanes(shape):
    return lax.broadcasted_iota(jnp.int32, shape, len(shape) - 1)


def parts(lev, cx):
    sizes, start, out = (cx, lev, lev, cx + 8, cx + 8), 0, []
    for size in sizes:
        out.append(pl.ds(start, size))
        start += size
    return out


def send_kernel(
    ndev, ngy, chunk, group, tile_source, tile_target, tile_row, mask, surface, weights, state,
    out, up, down, own,
    src, tgt, row, count, labels, mbuf, sbuf, wbuf, buf, sems, wsems, usems,
):
    lev, cx, cy = state.shape
    tiles = weights.shape[0]
    wet, up_near, down_near, left, right = (own.at[part] for part in parts(lev, cx))
    small = [
        pltpu.make_async_copy(a, b, sems.at[i])
        for i, (a, b) in enumerate(
            ((tile_source, src), (tile_target, tgt), (tile_row, row), (mask, mbuf), (surface, sbuf))
        )
    ]
    for copy in small:
        copy.start()
    wcopies, ucopies = [], []
    for i in range(tiles // chunk):
        part = pl.ds(i * chunk, chunk)
        wcopies.append(pltpu.make_async_copy(weights.at[part], wbuf.at[part], wsems.at[i]))
        wcopies[-1].start()
    for i in range(lev // group):
        part = pl.ds(i * group, group)
        ucopies.append(pltpu.make_async_copy(state.at[part], buf.at[part], usems.at[i]))
        ucopies[-1].start()
    out[...] = jnp.zeros_like(out)
    labels[...] = jnp.zeros_like(labels)
    for d in range(ndev):
        count[d] = 0
    me = lax.axis_index("gx") * ngy + lax.axis_index("gy")
    place = lax.broadcasted_iota(jnp.int32, (8, 128), 0) * 128 + lanes((8, 128))
    for copy in small:
        copy.wait()
    wet[...] = wet_of(mbuf)

    def one(t, _):
        s, d = src[t], tgt[t]
        rank = count[d]
        count[d] = rank + 1
        picked = sbuf[pl.ds(s, 8, stride=cx), :] * wet[pl.ds(s, 1), :]
        out[d, pl.ds(rank * 8, 8), :] = lax.dot_general(
            picked.astype(jnp.bfloat16),
            wbuf[t],
            (((1,), (1,)), ((), ())),
            preferred_element_type=jnp.float32,
        )
        label = (row[t] + 1).astype(jnp.float32)
        labels[d] = jnp.where(place == me * CAP + rank, label, labels[d])
        return 0

    for i in range(tiles // chunk):
        wcopies[i].wait()
        lax.fori_loop(i * chunk, (i + 1) * chunk, one, 0, unroll=True)
    for d in range(ndev):
        out[d, 64:72, :] = labels[d]

    turned = jnp.transpose(wet[...])
    up[2 * lev :, :] = jnp.broadcast_to(wet[0:1, :], (8, cy))
    down[2 * lev :, :] = jnp.broadcast_to(wet[cx - 1 :, :], (8, cy))
    left[cx:, :] = jnp.broadcast_to(turned[0:1, :], (8, cx))
    right[cx:, :] = jnp.broadcast_to(turned[cy - 1 :, :], (8, cx))
    strip = 32
    flat = buf.reshape(lev * cx, cy)
    lane = lanes((strip, cy))
    for i in range(lev // group):
        ucopies[i].wait()
        for dst, off, r in ((up, 0, 0), (up, lev, 1), (down, 0, cx - 1), (down, lev, cx - 2)):
            dst[pl.ds(off + i * group, group), :] = (
                flat[pl.ds(i * group * cx + r, group, stride=cx), :] * wet[r : r + 1, :]
            )
        for b in range(cx // strip):
            rows = pl.ds(b * strip, strip)
            if i == 0:
                lo = hi = jnp.zeros((strip, cy), jnp.float32)
            else:
                lo, hi = left[rows, :], right[rows, :]
            for l in range(i * group, (i + 1) * group):
                moved = pltpu.roll(buf[l, rows, :], (2 * l + 2) % cy, 1)
                at = (2 * l + 2) % cy
                lo = jnp.where((lane == at) | (lane == at + 1), moved, lo)
                hi = jnp.where((lane == 2 * l) | (lane == 2 * l + 1), moved, hi)
            if i == lev // group - 1:
                edge = wet[rows, :]
                first, second = edge[:, 0:1], edge[:, 1:2]
                lo = lo * jnp.where(lane % 2 == 0, first, second)
                first, second = edge[:, cy - 2 : cy - 1], edge[:, cy - 1 :]
                hi = hi * jnp.where(lane % 2 == 0, first, second)
            left[rows, :] = lo
            right[rows, :] = hi
    up_near[...] = up[0:lev, :]
    down_near[...] = down[0:lev, :]


def outgoing(tile_source, tile_target, tile_row, mask, surface, weights, state, ngx, ngy):
    tiles = weights.shape[0]
    lev, cx, cy = state.shape
    ndev, chunk, group = ngx * ngy, 32, lev
    message = jax.ShapeDtypeStruct((2 * lev + 8, cy), jnp.float32)
    return pl.pallas_call(
        functools.partial(send_kernel, ndev, ngy, chunk, group),
        out_shape=(
            jax.ShapeDtypeStruct((ndev, 72, 128), jnp.float32),
            message,
            message,
            jax.ShapeDtypeStruct((parts(lev, cx)[-1].start + cx + 8, cy), jnp.float32),
        ),
        in_specs=[ANY] * 7,
        out_specs=(VMEM,) * 4,
        scratch_shapes=[
            pltpu.SMEM((tiles,), jnp.int32),
            pltpu.SMEM((tiles,), jnp.int32),
            pltpu.SMEM((tiles,), jnp.int32),
            pltpu.SMEM((ndev,), jnp.int32),
            pltpu.VMEM((ndev, 8, 128), jnp.float32),
            pltpu.VMEM(mask.shape, jnp.int32),
            pltpu.VMEM(surface.shape, jnp.float32),
            pltpu.VMEM(weights.shape, weights.dtype),
            pltpu.VMEM(state.shape, jnp.float32),
            pltpu.SemaphoreType.DMA((5,)),
            pltpu.SemaphoreType.DMA((tiles // chunk,)),
            pltpu.SemaphoreType.DMA((lev // group,)),
        ],
        compiler_params=params(LIMIT),
        cost_estimate=pl.CostEstimate(flops=10**8, bytes_accessed=8 * 10**6, transcendentals=0),
    )(tile_source, tile_target, tile_row, mask, surface, weights, state)


def shifted(x, by, axis):
    size = x.shape[axis]
    moved = pltpu.roll(x, by % size, axis)
    index = lax.broadcasted_iota(jnp.int32, x.shape, axis)
    return jnp.where(index == (0 if by == 1 else size - 1), 0.0, moved)


PAD = 8


def relay_kernel(own, top, bottom, to_west, to_east):
    cx = to_west.shape[0] - 8
    cy = to_west.shape[1]
    lev = top.shape[0] // 2 - 4
    eye = lanes((lev, cy)) == lax.broadcasted_iota(jnp.int32, (lev, cy), 0)
    for out, part, c in ((to_west, parts(lev, cx)[3], 0), (to_east, parts(lev, cx)[4], cy - 1)):
        out[...] = own[part, :]
        for i, msg in enumerate((top, bottom)):
            column = msg[0:lev, c : c + 1]
            row = jnp.sum(jnp.where(eye, column, 0.0), axis=0, keepdims=True)
            out[cx + 1 + i : cx + 2 + i, :] = row


def relay(own, top, bottom, cx):
    cy = own.shape[1]
    columns = jax.ShapeDtypeStruct((cx + 8, cy), jnp.float32)
    return pl.pallas_call(
        relay_kernel,
        out_shape=(columns, columns),
        in_specs=[VMEM] * 3,
        out_specs=(VMEM, VMEM),
        compiler_params=params(8),
        cost_estimate=pl.CostEstimate(flops=10**11, bytes_accessed=10**8, transcendentals=0),
    )(own, top, bottom)


def ring_kernel(ngx, ngy, own, top, bottom, west, east, ring):
    cx, cy = west.shape[0] - 8, west.shape[1]
    lev = top.shape[0] // 2 - 4
    _, up, down, left, right = (own.at[part] for part in parts(lev, cx))
    ocean = lax.axis_index("mp") == 1
    horiz = jnp.where(ocean, HORIZ[1], HORIZ[0]).astype(jnp.float32)
    vert = jnp.where(ocean, VERT[1], VERT[0]).astype(jnp.float32)
    centre = 1.0 - 4.0 * horiz - 2.0 * vert
    gx, gy = lax.axis_index("gx"), lax.axis_index("gy")
    has = lambda c: jnp.where(c, 1.0, 0.0).astype(jnp.float32)
    has_top, has_bottom = has(gx > 0), has(gx < ngx - 1)
    has_west, has_east = has(gy > 0), has(gy < ngy - 1)

    lane = lanes((lev, cy))
    eye = lane == lax.broadcasted_iota(jnp.int32, (lev, cy), 0)

    def corner(msg, i, flag):
        row = msg[cx + 1 + i : cx + 2 + i, :]
        return flag * jnp.sum(jnp.where(eye, row, 0.0), axis=1, keepdims=True)

    corners = [
        (corner(west, i, flag * has_west), corner(east, i, flag * has_east))
        for i, flag in enumerate((has_top, has_bottom))
    ]
    for msg, mine, flag, i in ((top, up, has_top, 0), (bottom, down, has_bottom, 1)):
        near = msg[0:lev, :] * flag
        far = msg[lev : 2 * lev, :] * flag
        w_corner, e_corner = corners[i]
        side = pltpu.roll(jnp.where(lane == cy - 1, w_corner, near), 1, 1) + pltpu.roll(
            jnp.where(lane == 0, e_corner, near), cy - 1, 1
        )
        gain = msg[2 * lev : 2 * lev + 1, :] * (horiz * flag)
        outer = (
            centre * near
            + gain * (side + far + mine[...])
            + vert * (shifted(near, 1, 0) + shifted(near, -1, 0))
        )
        ring[2 * i * lev : (2 * i + 1) * lev, :] = near
        ring[(2 * i + 1) * lev : (2 * i + 2) * lev, :] = outer

    lane = lanes((cx, cy))
    odd = lane % 2 == 1
    west_cols = west[0:cx, :] * has_west
    east_cols = east[0:cx, :] * has_east
    w_gain = jnp.transpose(jnp.broadcast_to(west[cx : cx + 1, :], (cx, cx))) * (horiz * has_west)
    e_gain = jnp.transpose(jnp.broadcast_to(east[cx : cx + 1, :], (cx, cx))) * (horiz * has_east)
    merged = jnp.where(odd, west_cols, east_cols)
    ring[4 * lev : 4 * lev + cx, :] = pltpu.roll(jnp.where(odd, merged, pltpu.roll(merged, cy - 2, 1)), cy - 1, 1)
    beside = (
        jnp.where(odd, pltpu.roll(west_cols, 1, 1), pltpu.roll(east_cols, cy - 1, 1))
        + jnp.where(odd, pltpu.roll(left[0:cx, :], cy - 1, 1), pltpu.roll(right[0:cx, :], 1, 1))
    )
    offset = lane[0:lev, :] - 2 * lax.broadcasted_iota(jnp.int32, (lev, cy), 0)
    at_west, at_east = offset == 1, (offset == 2) | (offset == 2 - cy)
    beyond = [
        jnp.sum(jnp.where(at_west, w, 0.0) + jnp.where(at_east, e, 0.0), axis=0, keepdims=True)
        for w, e in corners
    ]
    sub = lax.broadcasted_iota(jnp.int32, (cx, cy), 0)
    above = jnp.where(sub == 0, beyond[0], pltpu.roll(merged, 1, 0))
    below = jnp.where(sub == cx - 1, beyond[1], pltpu.roll(merged, cx - 1, 0))
    less = jnp.where((lane == 1) | (lane == 2), 0.0, pltpu.roll(merged, 2, 1))
    more = jnp.where((lane == cy - 1) | (lane == 0), 0.0, pltpu.roll(merged, cy - 2, 1))
    merged = (
        centre * merged
        + jnp.where(odd, w_gain, e_gain) * (beside + above + below)
        + vert * (less + more)
    )
    ring[4 * lev + cx :, :] = pltpu.roll(jnp.where(odd, merged, pltpu.roll(merged, cy - 2, 1)), cy - 1, 1)


def outer_ring(own, top, bottom, west, east, ngx, ngy):
    cx, cy = west.shape[0] - 8, west.shape[1]
    lev = top.shape[0] // 2 - 4
    return pl.pallas_call(
        functools.partial(ring_kernel, ngx, ngy),
        out_shape=jax.ShapeDtypeStruct((4 * lev + 2 * cx, cy), jnp.float32),
        in_specs=[VMEM] * 5,
        out_specs=VMEM,
        compiler_params=params(8),
        cost_estimate=pl.CostEstimate(flops=10**6, bytes_accessed=10**5, transcendentals=0),
    )(own, top, bottom, west, east)


def stencil_kernel(
    group, own, state, ring, out, hwet, one, two, rbuf, res, sems, osems,
):
    lev, cx, cy = state.shape
    wet = own.at[pl.ds(0, cx)]
    pieces = lev // group
    fetch = pltpu.make_async_copy(ring, rbuf, sems.at[pieces])
    fetch.start()
    copies = []
    for i in range(pieces):
        part = pl.ds(i * group, group)
        copies.append(
            pltpu.make_async_copy(
                state.at[part], one.at[pl.ds(i * group + 1, group), pl.ds(PAD, cx), :], sems.at[i]
            )
        )
        copies[-1].start()
    ocean = lax.axis_index("mp") == 1
    horiz = jnp.where(ocean, HORIZ[1], HORIZ[0]).astype(jnp.float32)
    vert = jnp.where(ocean, VERT[1], VERT[0]).astype(jnp.float32)
    centre = 1.0 - 4.0 * horiz - 2.0 * vert
    hwet[...] = wet[...] * horiz
    lane = lanes((cx, cy))
    height = cx + 2 * PAD
    flat_one = one.reshape((lev + 2) * height, cy)
    flat_two = two.reshape((lev + 2) * height, cy)
    fetch.wait()
    for buf, off, at in (
        (flat_one, 0, PAD - 1),
        (flat_two, lev, PAD - 1),
        (flat_one, 2 * lev, PAD + cx),
        (flat_two, 3 * lev, PAD + cx),
    ):
        buf[pl.ds(height + at, lev, stride=height), :] = rbuf[off : off + lev, :]
    for buf in (one, two):
        buf[0] = jnp.zeros((height, cy), jnp.float32)
        buf[lev + 1] = jnp.zeros((height, cy), jnp.float32)

    def mask_level(l, _):
        one[l + 1, PAD : PAD + cx, :] = one[l + 1, PAD : PAD + cx, :] * wet[...]
        return 0

    ends = (lane == 0) | (lane == cy - 1)
    apart = lax.broadcasted_iota(jnp.int32, (cy, cy), 0) - lanes((cy, cy))
    pairs = jnp.where((apart == 1) | (apart == -1), 1.0, 0.0).astype(jnp.bfloat16)
    pairs = jnp.concatenate([pairs, pairs], axis=0)

    def beside_of(here):
        high = here.astype(jnp.bfloat16)
        low = (here - high.astype(jnp.float32)).astype(jnp.bfloat16)
        both = jnp.concatenate([high, low], axis=1)
        return jnp.dot(both, pairs, preferred_element_type=jnp.float32)

    def step(buf, sides, l, j):
        here = buf[l + 1, PAD : PAD + cx, :]
        edge = pltpu.roll(sides, (cy - 2 * j) % cy, 1)
        around = (
            jnp.where(ends, edge, 0.0)
            + beside_of(here)
            + buf[l + 1, PAD - 1 : PAD - 1 + cx, :]
            + buf[l + 1, PAD + 1 : PAD + 1 + cx, :]
        )
        column = buf[l, PAD : PAD + cx, :] + buf[l + 2, PAD : PAD + cx, :]
        return centre * here + hwet[...] * around + vert * column

    def first_levels(start, count, turn):
        sides = pltpu.roll(rbuf[4 * lev : 4 * lev + cx, :], lax.rem(2 * cy - 2 * start, cy), 1)
        for j in range(count):
            two[start + j + 1, PAD : PAD + cx, :] = step(one, sides, start + j, j)

    def second_levels(start, count):
        sides = pltpu.roll(rbuf[4 * lev + cx :, :], lax.rem(2 * cy - 2 * start, cy), 1)
        for j in range(count):
            res[start + j] = step(two, sides, start + j, j)

    def arrive(i):
        pltpu.make_async_copy(
            state.at[pl.ds(i * group, group)],
            one.at[pl.ds(i * group + 1, group), pl.ds(PAD, cx), :],
            sems.at[i],
        ).wait()
        for j in range(group):
            mask_level(i * group + j, 0)

    def leave(i):
        part = pl.ds(i * group, group)
        return pltpu.make_async_copy(res.at[part], out.at[part], osems.at[i])

    arrive(0)
    first_levels(0, group - 1, 0)

    def middle(i, _):
        arrive(i)
        first_levels(i * group - 1, group, 0)
        second_levels((i - 1) * group, group)
        leave(i - 1).start()
        return 0

    lax.fori_loop(1, pieces, middle, 0)
    first_levels(lev - 1, 1, 0)
    second_levels(lev - group, group)
    leave(pieces - 1).start()
    for i in range(pieces):
        leave(i).wait()


def two_steps(own, state, ring):
    lev, cx, cy = state.shape
    group = 8
    padded = (lev + 2, cx + 2 * PAD, cy)
    return pl.pallas_call(
        functools.partial(stencil_kernel, group),
        out_shape=jax.ShapeDtypeStruct(state.shape, jnp.float32),
        in_specs=[VMEM, ANY, ANY],
        out_specs=ANY,
        scratch_shapes=[
            pltpu.VMEM((cx, cy), jnp.float32),
            pltpu.VMEM(padded, jnp.float32),
            pltpu.VMEM(padded, jnp.float32),
            pltpu.VMEM(ring.shape, jnp.float32),
            pltpu.VMEM(state.shape, jnp.float32),
            pltpu.SemaphoreType.DMA((lev // group + 1,)),
            pltpu.SemaphoreType.DMA((lev // group,)),
        ],
        compiler_params=params(24),
        cost_estimate=pl.CostEstimate(flops=10**6, bytes_accessed=10**5, transcendentals=0),
    )(own, state, ring)


def collect_kernel(own, got, second, out, received, level, onehot, sums, sems, rsems):
    ndev = got.shape[0]
    fields, cx, cy = received.shape
    slots = ndev * CAP
    fetch = pltpu.make_async_copy(second.at[0], level, sems.at[0])
    fetch.start()
    store = pltpu.make_async_copy(level, out.at[0], sems.at[1])

    def leave(k):
        return pltpu.make_async_copy(sums.at[k], received.at[k], rsems.at[k])

    flat = got.reshape(ndev * 72, 128)
    labels = flat[64:72, :]
    for s in range(1, ndev):
        labels = labels + flat[s * 72 + 64 : s * 72 + 72, :]
    labels = labels.astype(jnp.int32)
    want = lax.broadcasted_iota(jnp.int32, (cx, 128), 0) + 1
    wide = jnp.concatenate([labels[q : q + 1, :] == want for q in range(slots // 128)], axis=1)
    hot = jnp.where(wide, 1.0, 0.0).astype(jnp.bfloat16)
    onehot[:, 0:slots] = hot
    onehot[:, slots:] = hot
    for k in range(fields):
        x = jnp.concatenate([flat[pl.ds(s * 72 + k, CAP, stride=8), :] for s in range(ndev)], axis=0)
        high = x.astype(jnp.bfloat16)
        low = (x - high.astype(jnp.float32)).astype(jnp.bfloat16)
        sums[k] = jnp.dot(
            onehot[...], jnp.concatenate([high, low], axis=0), preferred_element_type=jnp.float32
        )
        leave(k).start()
        if k == 0:
            fetch.wait()
            level[...] = level[...] + FORCE * own[0:cx, :] * sums[0]
            store.start()
    store.wait()
    for k in range(fields):
        leave(k).wait()


def collect(own, got, second, fields):
    ndev = got.shape[0]
    _, cx, cy = second.shape
    return pl.pallas_call(
        collect_kernel,
        out_shape=(
            jax.ShapeDtypeStruct(second.shape, jnp.float32),
            jax.ShapeDtypeStruct((fields, cx, cy), jnp.float32),
        ),
        in_specs=[VMEM, VMEM, ANY],
        out_specs=(ANY, ANY),
        scratch_shapes=[
            pltpu.VMEM((cx, cy), jnp.float32),
            pltpu.VMEM((cx, 2 * ndev * CAP), jnp.bfloat16),
            pltpu.VMEM((fields, cx, cy), jnp.float32),
            pltpu.SemaphoreType.DMA((2,)),
            pltpu.SemaphoreType.DMA((fields,)),
        ],
        input_output_aliases={2: 0},
        compiler_params=params(16),
        cost_estimate=pl.CostEstimate(flops=10**8, bytes_accessed=2 * 10**6, transcendentals=0),
    )(own, got, second)


def local(states, surface, land_mask, tile_weights, tile_source, tile_target, tile_row):
    ngx, ngy = lax.axis_size("gx"), lax.axis_size("gy")
    ndev = ngx * ngy
    state, fields = states[0], surface.shape[1]
    cx, cy = land_mask.shape
    ahead = lambda n: [(i, (i + 1) % n) for i in range(n)]
    behind = lambda n: [((i + 1) % n, i) for i in range(n)]
    buckets, up, down, own = outgoing(
        tile_source[0, 0, 0],
        tile_target[0, 0, 0, :, 0],
        tile_row[0, 0, 0],
        land_mask,
        surface.reshape(fields * cx, cy),
        tile_weights[0, 0, 0],
        state,
        ngx,
        ngy,
    )
    top = lax.ppermute(down, "gx", ahead(ngx))
    bottom = lax.ppermute(up, "gx", behind(ngx))
    buckets = lax.ppermute(buckets, "mp", [(0, 1), (1, 0)])
    got = lax.all_to_all(buckets, ("gx", "gy"), split_axis=0, concat_axis=0, tiled=True)
    to_west, to_east = relay(own, top, bottom, cx)
    west = lax.ppermute(to_east, "gy", ahead(ngy))
    east = lax.ppermute(to_west, "gy", behind(ngy))
    ring = outer_ring(own, top, bottom, west, east, ngx, ngy)
    second = two_steps(own, state, ring)
    new_state, received = collect(own, got, second, fields)
    return new_state[None], received[None]


def solution(mesh):
    return jax.shard_map(
        local,
        mesh=mesh,
        in_specs=(
            P("mp", None, "gx", "gy"),
            P("mp", None, "gx", "gy"),
            P("gx", "gy"),
            P("mp", "gx", "gy", None, None, None),
            P("mp", "gx", "gy", None),
            P("mp", "gx", "gy", None, None),
            P("mp", "gx", "gy", None),
        ),
        out_specs=(P("mp", None, "gx", "gy"), P("mp", None, "gx", "gy")),
        check_vma=False,
    )
```

```python
import functools

import jax
import jax.numpy as jnp
from jax import lax
from jax.experimental import pallas as pl
from jax.experimental.pallas import tpu as pltpu
from jax.sharding import PartitionSpec as P

CAP = 8
FORCE = 0.5
HORIZ = (0.15, 0.12)
VERT = (0.1, 0.15)
MIB = 1024 * 1024
LIMIT = 60
FIRST_COST = 5 * 10**9
ANY = pl.BlockSpec(memory_space=pl.ANY)
VMEM = pl.BlockSpec(memory_space=pltpu.VMEM)
SMEM = pl.BlockSpec(memory_space=pltpu.SMEM)


def params(mib):
    return pltpu.CompilerParams(vmem_limit_bytes=mib * MIB)


def wet_of(mask_ref):
    ocean = lax.axis_index("mp") == 1
    return jnp.where(ocean, mask_ref[...].astype(jnp.float32), 1.0)


def lanes(shape):
    return lax.broadcasted_iota(jnp.int32, shape, len(shape) - 1)


def parts(lev, cx):
    sizes, start, out = (cx, lev, lev, cx + 8, cx + 8), 0, []
    for size in sizes:
        out.append(pl.ds(start, size))
        start += size
    return out


def send_kernel(
    ndev, ngy, chunk, group, tile_source, tile_target, tile_row, mask, surface, weights, state,
    out, up, down, own,
    src, tgt, row, count, labels, mbuf, sbuf, wbuf, buf, sems, wsems, usems,
):
    lev, cx, cy = state.shape
    tiles = weights.shape[0]
    wet, up_near, down_near, left, right = (own.at[part] for part in parts(lev, cx))
    small = [
        pltpu.make_async_copy(a, b, sems.at[i])
        for i, (a, b) in enumerate(
            ((tile_source, src), (tile_target, tgt), (tile_row, row), (mask, mbuf), (surface, sbuf))
        )
    ]
    for copy in small:
        copy.start()
    wcopies, ucopies = [], []
    for i in range(tiles // chunk):
        part = pl.ds(i * chunk, chunk)
        wcopies.append(pltpu.make_async_copy(weights.at[part], wbuf.at[part], wsems.at[i]))
        wcopies[-1].start()
    for i in range(lev // group):
        part = pl.ds(i * group, group)
        ucopies.append(pltpu.make_async_copy(state.at[part], buf.at[part], usems.at[i]))
        ucopies[-1].start()
    block = out.shape[0] // ndev
    extra = block - 8 * CAP
    out[...] = jnp.zeros_like(out)
    labels[...] = jnp.zeros_like(labels)
    for d in range(ndev):
        count[d] = 0
    me = lax.axis_index("gx") * ngy + lax.axis_index("gy")
    place = lax.broadcasted_iota(jnp.int32, (8, 128), 0) * 128 + lanes((8, 128))
    for copy in small:
        copy.wait()
    wet[...] = wet_of(mbuf)

    def one(t, _):
        s, d = src[t], tgt[t]
        rank = count[d]
        count[d] = rank + 1
        picked = sbuf[pl.ds(s, 8, stride=cx), :] * wet[pl.ds(s, 1), :]
        out[pl.ds(d * block + rank * 8, 8), :] = lax.dot_general(
            picked.astype(jnp.bfloat16),
            wbuf[t],
            (((1,), (1,)), ((), ())),
            preferred_element_type=jnp.float32,
        )
        label = (row[t] + 1).astype(jnp.float32)
        labels[d] = jnp.where(place == me * CAP + rank, label, labels[d])
        return 0

    for i in range(tiles // chunk):
        wcopies[i].wait()
        lax.fori_loop(i * chunk, (i + 1) * chunk, one, 0, unroll=True)
    for d in range(ndev):
        out[(d + 1) * block - extra : (d + 1) * block, :] = labels[d, 0:extra, :]

    turned = jnp.transpose(wet[...])
    up[2 * lev :, :] = jnp.broadcast_to(wet[0:1, :], (8, cy))
    down[2 * lev :, :] = jnp.broadcast_to(wet[cx - 1 :, :], (8, cy))
    left[cx:, :] = jnp.broadcast_to(turned[0:1, :], (8, cx))
    right[cx:, :] = jnp.broadcast_to(turned[cy - 1 :, :], (8, cx))
    strip = 32
    flat = buf.reshape(lev * cx, cy)
    lane = lanes((strip, cy))
    for i in range(lev // group):
        ucopies[i].wait()
        for dst, off, r in ((up, 0, 0), (up, lev, 1), (down, 0, cx - 1), (down, lev, cx - 2)):
            dst[pl.ds(off + i * group, group), :] = (
                flat[pl.ds(i * group * cx + r, group, stride=cx), :] * wet[r : r + 1, :]
            )
        for b in range(cx // strip):
            rows = pl.ds(b * strip, strip)
            if i == 0:
                lo = hi = jnp.zeros((strip, cy), jnp.float32)
            else:
                lo, hi = left[rows, :], right[rows, :]
            for l in range(i * group, (i + 1) * group):
                moved = pltpu.roll(buf[l, rows, :], (2 * l + 2) % cy, 1)
                at = (2 * l + 2) % cy
                lo = jnp.where((lane == at) | (lane == at + 1), moved, lo)
                hi = jnp.where((lane == 2 * l) | (lane == 2 * l + 1), moved, hi)
            if i == lev // group - 1:
                edge = wet[rows, :]
                first, second = edge[:, 0:1], edge[:, 1:2]
                lo = lo * jnp.where(lane % 2 == 0, first, second)
                first, second = edge[:, cy - 2 : cy - 1], edge[:, cy - 1 :]
                hi = hi * jnp.where(lane % 2 == 0, first, second)
            left[rows, :] = lo
            right[rows, :] = hi
    up_near[...] = up[0:lev, :]
    down_near[...] = down[0:lev, :]


def outgoing(tile_source, tile_target, tile_row, mask, surface, weights, state, ngx, ngy):
    tiles = weights.shape[0]
    lev, cx, cy = state.shape
    ndev, chunk, group = ngx * ngy, 32, lev
    block = 8 * CAP + ndev * CAP // 128
    message = jax.ShapeDtypeStruct((2 * lev + 8, cy), jnp.float32)
    return pl.pallas_call(
        functools.partial(send_kernel, ndev, ngy, chunk, group),
        out_shape=(
            jax.ShapeDtypeStruct((ndev * block, 128), jnp.float32),
            message,
            message,
            jax.ShapeDtypeStruct((parts(lev, cx)[-1].start + cx + 8, cy), jnp.float32),
        ),
        in_specs=[ANY] * 7,
        out_specs=(VMEM,) * 4,
        scratch_shapes=[
            pltpu.SMEM((tiles,), jnp.int32),
            pltpu.SMEM((tiles,), jnp.int32),
            pltpu.SMEM((tiles,), jnp.int32),
            pltpu.SMEM((ndev,), jnp.int32),
            pltpu.VMEM((ndev, 8, 128), jnp.float32),
            pltpu.VMEM(mask.shape, jnp.int32),
            pltpu.VMEM(surface.shape, jnp.float32),
            pltpu.VMEM(weights.shape, weights.dtype),
            pltpu.VMEM(state.shape, jnp.float32),
            pltpu.SemaphoreType.DMA((5,)),
            pltpu.SemaphoreType.DMA((tiles // chunk,)),
            pltpu.SemaphoreType.DMA((lev // group,)),
        ],
        compiler_params=params(LIMIT),
        cost_estimate=pl.CostEstimate(flops=10**8, bytes_accessed=8 * 10**6, transcendentals=0),
    )(tile_source, tile_target, tile_row, mask, surface, weights, state)


def shifted(x, by, axis):
    size = x.shape[axis]
    moved = pltpu.roll(x, by % size, axis)
    index = lax.broadcasted_iota(jnp.int32, x.shape, axis)
    return jnp.where(index == (0 if by == 1 else size - 1), 0.0, moved)


PAD = 8


def relay_kernel(own, top, bottom, to_west, to_east):
    cx = to_west.shape[0] - 8
    cy = to_west.shape[1]
    lev = top.shape[0] // 2 - 4
    eye = lanes((lev, cy)) == lax.broadcasted_iota(jnp.int32, (lev, cy), 0)
    for out, part, c in ((to_west, parts(lev, cx)[3], 0), (to_east, parts(lev, cx)[4], cy - 1)):
        out[...] = own[part, :]
        for i, msg in enumerate((top, bottom)):
            column = msg[0:lev, c : c + 1]
            row = jnp.sum(jnp.where(eye, column, 0.0), axis=0, keepdims=True)
            out[cx + 1 + i : cx + 2 + i, :] = row


def relay(own, top, bottom, cx):
    cy = own.shape[1]
    columns = jax.ShapeDtypeStruct((cx + 8, cy), jnp.float32)
    return pl.pallas_call(
        relay_kernel,
        out_shape=(columns, columns),
        in_specs=[VMEM] * 3,
        out_specs=(VMEM, VMEM),
        compiler_params=params(8),
        cost_estimate=pl.CostEstimate(flops=10**11, bytes_accessed=10**8, transcendentals=0),
    )(own, top, bottom)


def ring_kernel(ngx, ngy, own, top, bottom, west, east, ring):
    cx, cy = west.shape[0] - 8, west.shape[1]
    lev = top.shape[0] // 2 - 4
    wet, up, down, left, right = (own.at[part] for part in parts(lev, cx))
    ocean = lax.axis_index("mp") == 1
    horiz = jnp.where(ocean, HORIZ[1], HORIZ[0]).astype(jnp.float32)
    vert = jnp.where(ocean, VERT[1], VERT[0]).astype(jnp.float32)
    centre = 1.0 - 4.0 * horiz - 2.0 * vert
    gx, gy = lax.axis_index("gx"), lax.axis_index("gy")
    has = lambda c: jnp.where(c, 1.0, 0.0).astype(jnp.float32)
    has_top, has_bottom = has(gx > 0), has(gx < ngx - 1)
    has_west, has_east = has(gy > 0), has(gy < ngy - 1)

    lane = lanes((lev, cy))
    eye = lane == lax.broadcasted_iota(jnp.int32, (lev, cy), 0)

    def corner(msg, i, flag):
        row = msg[cx + 1 + i : cx + 2 + i, :]
        return flag * jnp.sum(jnp.where(eye, row, 0.0), axis=1, keepdims=True)

    corners = [
        (corner(west, i, flag * has_west), corner(east, i, flag * has_east))
        for i, flag in enumerate((has_top, has_bottom))
    ]
    for msg, mine, flag, i in ((top, up, has_top, 0), (bottom, down, has_bottom, 1)):
        near = msg[0:lev, :] * flag
        far = msg[lev : 2 * lev, :] * flag
        w_corner, e_corner = corners[i]
        side = pltpu.roll(jnp.where(lane == cy - 1, w_corner, near), 1, 1) + pltpu.roll(
            jnp.where(lane == 0, e_corner, near), cy - 1, 1
        )
        gain = msg[2 * lev : 2 * lev + 1, :] * (horiz * flag)
        outer = (
            centre * near
            + gain * (side + far + mine[...])
            + vert * (shifted(near, 1, 0) + shifted(near, -1, 0))
        )
        ring[i * lev : (i + 1) * lev, :] = outer

    lane = lanes((cx, cy))
    odd = lane % 2 == 1
    west_cols = west[0:cx, :] * has_west
    east_cols = east[0:cx, :] * has_east
    w_gain = jnp.transpose(jnp.broadcast_to(west[cx : cx + 1, :], (cx, cx))) * (horiz * has_west)
    e_gain = jnp.transpose(jnp.broadcast_to(east[cx : cx + 1, :], (cx, cx))) * (horiz * has_east)
    merged = jnp.where(odd, west_cols, east_cols)
    given = merged * (horiz * jnp.where(odd, wet[:, 0:1], wet[:, cy - 1 : cy]))
    ring[2 * lev : 2 * lev + cx, :] = pltpu.roll(
        jnp.where(odd, given, pltpu.roll(given, cy - 2, 1)), cy - 1, 1
    )
    beside = (
        jnp.where(odd, pltpu.roll(west_cols, 1, 1), pltpu.roll(east_cols, cy - 1, 1))
        + jnp.where(odd, pltpu.roll(left[0:cx, :], cy - 1, 1), pltpu.roll(right[0:cx, :], 1, 1))
    )
    offset = lane[0:lev, :] - 2 * lax.broadcasted_iota(jnp.int32, (lev, cy), 0)
    at_west, at_east = offset == 1, (offset == 2) | (offset == 2 - cy)
    beyond = [
        jnp.sum(jnp.where(at_west, w, 0.0) + jnp.where(at_east, e, 0.0), axis=0, keepdims=True)
        for w, e in corners
    ]
    sub = lax.broadcasted_iota(jnp.int32, (cx, cy), 0)
    above = jnp.where(sub == 0, beyond[0], pltpu.roll(merged, 1, 0))
    below = jnp.where(sub == cx - 1, beyond[1], pltpu.roll(merged, cx - 1, 0))
    less = jnp.where((lane == 1) | (lane == 2), 0.0, pltpu.roll(merged, 2, 1))
    more = jnp.where((lane == cy - 1) | (lane == 0), 0.0, pltpu.roll(merged, cy - 2, 1))
    merged = (
        centre * merged
        + jnp.where(odd, w_gain, e_gain) * (beside + above + below)
        + vert * (less + more)
    )
    ring[2 * lev + cx :, :] = pltpu.roll(jnp.where(odd, merged, pltpu.roll(merged, cy - 2, 1)), cy - 1, 1)


def outer_ring(own, top, bottom, west, east, ngx, ngy):
    cx, cy = west.shape[0] - 8, west.shape[1]
    lev = top.shape[0] // 2 - 4
    return pl.pallas_call(
        functools.partial(ring_kernel, ngx, ngy),
        out_shape=jax.ShapeDtypeStruct((2 * lev + 2 * cx, cy), jnp.float32),
        in_specs=[VMEM] * 5,
        out_specs=VMEM,
        compiler_params=params(8),
        cost_estimate=pl.CostEstimate(flops=10**6, bytes_accessed=10**5, transcendentals=0),
    )(own, top, bottom, west, east)


def step_kernel(ngx, group, second, own, x, *refs):
    if second:
        ring, out, hwet, buf, res, sems, osems = refs
    else:
        top, bottom, out, hwet, buf, res, sems, osems = refs
    lev, cx, cy = x.shape
    pieces = lev // group

    def arrive(i):
        return pltpu.make_async_copy(
            x.at[pl.ds(i * group, group)],
            buf.at[pl.ds(i * group + 1, group), pl.ds(PAD, cx), :],
            sems.at[i],
        )

    def leave(i):
        part = pl.ds(i * group, group)
        return pltpu.make_async_copy(res.at[part], out.at[part], osems.at[i])

    for i in range(pieces):
        arrive(i).start()
    ocean = lax.axis_index("mp") == 1
    horiz = jnp.where(ocean, HORIZ[1], HORIZ[0]).astype(jnp.float32)
    vert = jnp.where(ocean, VERT[1], VERT[0]).astype(jnp.float32)
    centre = 1.0 - 4.0 * horiz - 2.0 * vert
    wet = own.at[pl.ds(0, cx)]
    hwet[...] = wet[...] * horiz
    lane = lanes((cx, cy))
    ends = (lane == 0) | (lane == cy - 1)
    height = cx + 2 * PAD
    flat = buf.reshape((lev + 2) * height, cy)
    above, below = pl.ds(height + PAD - 1, lev, stride=height), pl.ds(height + PAD + cx, lev, stride=height)
    if second:
        flat[above, :] = ring[0:lev, :]
        flat[below, :] = ring[lev : 2 * lev, :]
    else:
        gx = lax.axis_index("gx")
        flat[above, :] = top[0:lev, :] * jnp.where(gx > 0, 1.0, 0.0).astype(jnp.float32)
        flat[below, :] = bottom[0:lev, :] * jnp.where(gx < ngx - 1, 1.0, 0.0).astype(jnp.float32)
    buf[0] = jnp.zeros((height, cy), jnp.float32)
    buf[lev + 1] = jnp.zeros((height, cy), jnp.float32)

    apart = lax.broadcasted_iota(jnp.int32, (cy, cy), 0) - lanes((cy, cy))
    pairs = jnp.where((apart == 1) | (apart == -1), 1.0, 0.0).astype(jnp.bfloat16)
    pairs = jnp.concatenate([pairs, pairs], axis=0)

    def beside_of(here):
        high = here.astype(jnp.bfloat16)
        low = (here - high.astype(jnp.float32)).astype(jnp.bfloat16)
        both = jnp.concatenate([high, low], axis=1)
        return jnp.dot(both, pairs, preferred_element_type=jnp.float32)

    def columns(part, start):
        off = 2 * lev + part * cx
        return pltpu.roll(ring[off : off + cx, :], lax.rem(2 * cy - 2 * start, cy), 1)

    def at_ends(sides, j):
        return jnp.where(ends, pltpu.roll(sides, (cy - 2 * j) % cy, 1), 0.0)

    def accept(i):
        arrive(i).wait()
        sides = columns(0, i * group) if second else None
        for j in range(group):
            here = (i * group + j + 1, slice(PAD, PAD + cx), slice(None))
            if second:
                buf[here] = buf[here] + at_ends(sides, j)
            else:
                buf[here] = buf[here] * wet[...]

    def levels(start, count):
        sides = columns(1, start) if second else None
        for j in range(count):
            l = start + j
            here = buf[l + 1, PAD : PAD + cx, :]
            around = (
                beside_of(here)
                + buf[l + 1, PAD - 1 : PAD - 1 + cx, :]
                + buf[l + 1, PAD + 1 : PAD + 1 + cx, :]
            )
            if second:
                around = around + at_ends(sides, j)
            column = buf[l, PAD : PAD + cx, :] + buf[l + 2, PAD : PAD + cx, :]
            res[l] = centre * here + hwet[...] * around + vert * column

    accept(0)
    levels(0, group - 1)

    def middle(i, _):
        accept(i)
        levels(i * group - 1, group)
        leave(i - 1).start()
        return 0

    lax.fori_loop(1, pieces, middle, 0)
    levels(lev - 1, 1)
    leave(pieces - 1).start()
    for i in range(pieces):
        leave(i).wait()


def one_step(own, x, outside, ngx, second):
    lev, cx, cy = x.shape
    group = 8
    return pl.pallas_call(
        functools.partial(step_kernel, ngx, group, second),
        out_shape=jax.ShapeDtypeStruct(x.shape, jnp.float32),
        in_specs=[VMEM, ANY] + [VMEM] * len(outside),
        out_specs=ANY,
        scratch_shapes=[
            pltpu.VMEM((cx, cy), jnp.float32),
            pltpu.VMEM((lev + 2, cx + 2 * PAD, cy), jnp.float32),
            pltpu.VMEM(x.shape, jnp.float32),
            pltpu.SemaphoreType.DMA((lev // group,)),
            pltpu.SemaphoreType.DMA((lev // group,)),
        ],
        compiler_params=params(16),
        cost_estimate=pl.CostEstimate(
            flops=10**6 if second else FIRST_COST, bytes_accessed=10**5, transcendentals=0
        ),
    )(own, x, *outside)


def collect_kernel(ndev, own, got, second, out, received, level, onehot, sums, sems, rsems):
    block = got.shape[0] // ndev
    extra = block - 8 * CAP
    fields, cx, cy = received.shape
    slots = ndev * CAP
    fetch = pltpu.make_async_copy(second.at[0], level, sems.at[0])
    fetch.start()
    store = pltpu.make_async_copy(level, out.at[0], sems.at[1])

    def leave(k):
        return pltpu.make_async_copy(sums.at[k], received.at[k], rsems.at[k])

    labels = got[block - extra : block, :]
    for s in range(1, ndev):
        labels = labels + got[(s + 1) * block - extra : (s + 1) * block, :]
    labels = labels.astype(jnp.int32)
    want = lax.broadcasted_iota(jnp.int32, (cx, 128), 0) + 1
    wide = jnp.concatenate([labels[q : q + 1, :] == want for q in range(slots // 128)], axis=1)
    hot = jnp.where(wide, 1.0, 0.0).astype(jnp.bfloat16)
    onehot[:, 0:slots] = hot
    onehot[:, slots:] = hot
    for k in range(fields):
        x = jnp.concatenate([got[pl.ds(s * block + k, CAP, stride=8), :] for s in range(ndev)], axis=0)
        high = x.astype(jnp.bfloat16)
        low = (x - high.astype(jnp.float32)).astype(jnp.bfloat16)
        sums[k] = jnp.dot(
            onehot[...], jnp.concatenate([high, low], axis=0), preferred_element_type=jnp.float32
        )
        leave(k).start()
        if k == 0:
            fetch.wait()
            level[...] = level[...] + FORCE * own[0:cx, :] * sums[0]
            store.start()
    store.wait()
    for k in range(fields):
        leave(k).wait()


def collect(own, got, second, fields, ndev):
    _, cx, cy = second.shape
    return pl.pallas_call(
        functools.partial(collect_kernel, ndev),
        out_shape=(
            jax.ShapeDtypeStruct(second.shape, jnp.float32),
            jax.ShapeDtypeStruct((fields, cx, cy), jnp.float32),
        ),
        in_specs=[VMEM, VMEM, ANY],
        out_specs=(ANY, ANY),
        scratch_shapes=[
            pltpu.VMEM((cx, cy), jnp.float32),
            pltpu.VMEM((cx, 2 * ndev * CAP), jnp.bfloat16),
            pltpu.VMEM((fields, cx, cy), jnp.float32),
            pltpu.SemaphoreType.DMA((2,)),
            pltpu.SemaphoreType.DMA((fields,)),
        ],
        input_output_aliases={2: 0},
        compiler_params=params(16),
        cost_estimate=pl.CostEstimate(flops=10**8, bytes_accessed=2 * 10**6, transcendentals=0),
    )(own, got, second)


def local(states, surface, land_mask, tile_weights, tile_source, tile_target, tile_row):
    ngx, ngy = lax.axis_size("gx"), lax.axis_size("gy")
    ndev = ngx * ngy
    state, fields = states[0], surface.shape[1]
    cx, cy = land_mask.shape
    ahead = lambda n: [(i, (i + 1) % n) for i in range(n)]
    behind = lambda n: [((i + 1) % n, i) for i in range(n)]
    buckets, up, down, own = outgoing(
        tile_source[0, 0, 0],
        tile_target[0, 0, 0, :, 0],
        tile_row[0, 0, 0],
        land_mask,
        surface.reshape(fields * cx, cy),
        tile_weights[0, 0, 0],
        state,
        ngx,
        ngy,
    )
    top = lax.ppermute(down, "gx", ahead(ngx))
    bottom = lax.ppermute(up, "gx", behind(ngx))
    buckets = lax.ppermute(buckets, "mp", [(0, 1), (1, 0)])
    whole = buckets.shape
    buckets = buckets.reshape(ndev, whole[0] // ndev, 1, whole[1])
    got = lax.all_to_all(buckets, ("gx", "gy"), split_axis=0, concat_axis=0, tiled=True)
    got = got.reshape(whole)
    to_west, to_east = relay(own, top, bottom, cx)
    west = lax.ppermute(to_east, "gy", ahead(ngy))
    east = lax.ppermute(to_west, "gy", behind(ngy))
    first = one_step(own, state, (top, bottom), ngx, False)
    ring = outer_ring(own, top, bottom, west, east, ngx, ngy)
    second = one_step(own, first, (ring,), ngx, True)
    new_state, received = collect(own, got, second, fields, ndev)
    return new_state[None], received[None]


def solution(mesh):
    return jax.shard_map(
        local,
        mesh=mesh,
        in_specs=(
            P("mp", None, "gx", "gy"),
            P("mp", None, "gx", "gy"),
            P("gx", "gy"),
            P("mp", "gx", "gy", None, None, None),
            P("mp", "gx", "gy", None),
            P("mp", "gx", "gy", None, None),
            P("mp", "gx", "gy", None),
        ),
        out_specs=(P("mp", None, "gx", "gy"), P("mp", None, "gx", "gy")),
        check_vma=False,
    )
```

```python
import functools

import jax
import jax.numpy as jnp
from jax import lax
from jax.experimental import pallas as pl
from jax.experimental.pallas import tpu as pltpu
from jax.sharding import PartitionSpec as P

CAP = 8
FORCE = 0.5
HORIZ = (0.15, 0.12)
VERT = (0.1, 0.15)
MIB = 1024 * 1024
LIMIT = 60
FIRST_COST = 5 * 10**9
ANY = pl.BlockSpec(memory_space=pl.ANY)
VMEM = pl.BlockSpec(memory_space=pltpu.VMEM)
SMEM = pl.BlockSpec(memory_space=pltpu.SMEM)


def params(mib):
    return pltpu.CompilerParams(vmem_limit_bytes=mib * MIB)


def wet_of(mask_ref):
    ocean = lax.axis_index("mp") == 1
    return jnp.where(ocean, mask_ref[...].astype(jnp.float32), 1.0)


def lanes(shape):
    return lax.broadcasted_iota(jnp.int32, shape, len(shape) - 1)


def parts(lev, cx):
    sizes, start, out = (cx, lev, lev, cx + 8, cx + 8), 0, []
    for size in sizes:
        out.append(pl.ds(start, size))
        start += size
    return out


def send_kernel(
    ndev, ngy, chunk, group, tile_source, tile_target, tile_row, mask, surface, weights, state,
    out, up, down, own,
    src, tgt, row, count, labels, mbuf, sbuf, wbuf, buf, sems, wsems, usems,
):
    lev, cx, cy = state.shape
    tiles = weights.shape[0]
    wet, up_near, down_near, left, right = (own.at[part] for part in parts(lev, cx))
    small = [
        pltpu.make_async_copy(a, b, sems.at[i])
        for i, (a, b) in enumerate(
            ((tile_source, src), (tile_target, tgt), (tile_row, row), (mask, mbuf), (surface, sbuf))
        )
    ]
    for copy in small:
        copy.start()
    wcopies, ucopies = [], []
    for i in range(tiles // chunk):
        part = pl.ds(i * chunk, chunk)
        wcopies.append(pltpu.make_async_copy(weights.at[part], wbuf.at[part], wsems.at[i]))
        wcopies[-1].start()
    for i in range(lev // group):
        part = pl.ds(i * group, group)
        ucopies.append(pltpu.make_async_copy(state.at[part], buf.at[part], usems.at[i]))
        ucopies[-1].start()
    block = out.shape[0] // ndev
    extra = block - 8 * CAP
    out[...] = jnp.zeros_like(out)
    labels[...] = jnp.zeros_like(labels)
    for d in range(ndev):
        count[d] = 0
    me = lax.axis_index("gx") * ngy + lax.axis_index("gy")
    place = lax.broadcasted_iota(jnp.int32, (8, 128), 0) * 128 + lanes((8, 128))
    for copy in small:
        copy.wait()
    wet[...] = wet_of(mbuf)

    def one(t, _):
        s, d = src[t], tgt[t]
        rank = count[d]
        count[d] = rank + 1
        picked = sbuf[pl.ds(s, 8, stride=cx), :] * wet[pl.ds(s, 1), :]
        out[pl.ds(d * block + rank * 8, 8), :] = lax.dot_general(
            picked.astype(jnp.bfloat16),
            wbuf[t],
            (((1,), (1,)), ((), ())),
            preferred_element_type=jnp.float32,
        )
        label = (row[t] + 1).astype(jnp.float32)
        labels[d] = jnp.where(place == me * CAP + rank, label, labels[d])
        return 0

    for i in range(tiles // chunk):
        wcopies[i].wait()
        lax.fori_loop(i * chunk, (i + 1) * chunk, one, 0, unroll=True)
    for d in range(ndev):
        out[(d + 1) * block - extra : (d + 1) * block, :] = labels[d, 0:extra, :]

    turned = jnp.transpose(wet[...])
    up[2 * lev :, :] = jnp.broadcast_to(wet[0:1, :], (8, cy))
    down[2 * lev :, :] = jnp.broadcast_to(wet[cx - 1 :, :], (8, cy))
    left[cx:, :] = jnp.broadcast_to(turned[0:1, :], (8, cx))
    right[cx:, :] = jnp.broadcast_to(turned[cy - 1 :, :], (8, cx))
    strip = 32
    flat = buf.reshape(lev * cx, cy)
    lane = lanes((strip, cy))
    for i in range(lev // group):
        ucopies[i].wait()
        for dst, off, r in ((up, 0, 0), (up, lev, 1), (down, 0, cx - 1), (down, lev, cx - 2)):
            dst[pl.ds(off + i * group, group), :] = (
                flat[pl.ds(i * group * cx + r, group, stride=cx), :] * wet[r : r + 1, :]
            )
        for b in range(cx // strip):
            rows = pl.ds(b * strip, strip)
            if i == 0:
                lo = hi = jnp.zeros((strip, cy), jnp.float32)
            else:
                lo, hi = left[rows, :], right[rows, :]
            for l in range(i * group, (i + 1) * group):
                moved = pltpu.roll(buf[l, rows, :], (2 * l + 2) % cy, 1)
                at = (2 * l + 2) % cy
                lo = jnp.where((lane == at) | (lane == at + 1), moved, lo)
                hi = jnp.where((lane == 2 * l) | (lane == 2 * l + 1), moved, hi)
            if i == lev // group - 1:
                edge = wet[rows, :]
                first, second = edge[:, 0:1], edge[:, 1:2]
                lo = lo * jnp.where(lane % 2 == 0, first, second)
                first, second = edge[:, cy - 2 : cy - 1], edge[:, cy - 1 :]
                hi = hi * jnp.where(lane % 2 == 0, first, second)
            left[rows, :] = lo
            right[rows, :] = hi
    up_near[...] = up[0:lev, :]
    down_near[...] = down[0:lev, :]


def outgoing(tile_source, tile_target, tile_row, mask, surface, weights, state, ngx, ngy):
    tiles = weights.shape[0]
    lev, cx, cy = state.shape
    ndev, chunk, group = ngx * ngy, 32, lev
    block = 8 * CAP + ndev * CAP // 128
    message = jax.ShapeDtypeStruct((2 * lev + 8, cy), jnp.float32)
    return pl.pallas_call(
        functools.partial(send_kernel, ndev, ngy, chunk, group),
        out_shape=(
            jax.ShapeDtypeStruct((ndev * block, 128), jnp.float32),
            message,
            message,
            jax.ShapeDtypeStruct((parts(lev, cx)[-1].start + cx + 8, cy), jnp.float32),
        ),
        in_specs=[ANY] * 7,
        out_specs=(VMEM,) * 4,
        scratch_shapes=[
            pltpu.SMEM((tiles,), jnp.int32),
            pltpu.SMEM((tiles,), jnp.int32),
            pltpu.SMEM((tiles,), jnp.int32),
            pltpu.SMEM((ndev,), jnp.int32),
            pltpu.VMEM((ndev, 8, 128), jnp.float32),
            pltpu.VMEM(mask.shape, jnp.int32),
            pltpu.VMEM(surface.shape, jnp.float32),
            pltpu.VMEM(weights.shape, weights.dtype),
            pltpu.VMEM(state.shape, jnp.float32),
            pltpu.SemaphoreType.DMA((5,)),
            pltpu.SemaphoreType.DMA((tiles // chunk,)),
            pltpu.SemaphoreType.DMA((lev // group,)),
        ],
        compiler_params=params(16),
        cost_estimate=pl.CostEstimate(flops=10**8, bytes_accessed=8 * 10**6, transcendentals=0),
    )(
        *[
            pltpu.with_memory_space_constraint(x, pltpu.HBM)
            for x in (tile_source, tile_target, tile_row, mask, surface, weights, state)
        ]
    )


def shifted(x, by, axis):
    size = x.shape[axis]
    moved = pltpu.roll(x, by % size, axis)
    index = lax.broadcasted_iota(jnp.int32, x.shape, axis)
    return jnp.where(index == (0 if by == 1 else size - 1), 0.0, moved)


PAD = 8


def relay_kernel(own, top, bottom, to_west, to_east):
    cx = to_west.shape[0] - 8
    cy = to_west.shape[1]
    lev = top.shape[0] // 2 - 4
    eye = lanes((lev, cy)) == lax.broadcasted_iota(jnp.int32, (lev, cy), 0)
    for out, part, c in ((to_west, parts(lev, cx)[3], 0), (to_east, parts(lev, cx)[4], cy - 1)):
        out[...] = own[part, :]
        for i, msg in enumerate((top, bottom)):
            column = msg[0:lev, c : c + 1]
            row = jnp.sum(jnp.where(eye, column, 0.0), axis=0, keepdims=True)
            out[cx + 1 + i : cx + 2 + i, :] = row


def relay(own, top, bottom, cx):
    cy = own.shape[1]
    columns = jax.ShapeDtypeStruct((cx + 8, cy), jnp.float32)
    return pl.pallas_call(
        relay_kernel,
        out_shape=(columns, columns),
        in_specs=[VMEM] * 3,
        out_specs=(VMEM, VMEM),
        compiler_params=params(8),
        cost_estimate=pl.CostEstimate(flops=10**11, bytes_accessed=10**8, transcendentals=0),
    )(own, top, bottom)


def ring_kernel(ngx, ngy, own, top, bottom, west, east, ring):
    cx, cy = west.shape[0] - 8, west.shape[1]
    lev = top.shape[0] // 2 - 4
    wet, up, down, left, right = (own.at[part] for part in parts(lev, cx))
    ocean = lax.axis_index("mp") == 1
    horiz = jnp.where(ocean, HORIZ[1], HORIZ[0]).astype(jnp.float32)
    vert = jnp.where(ocean, VERT[1], VERT[0]).astype(jnp.float32)
    centre = 1.0 - 4.0 * horiz - 2.0 * vert
    gx, gy = lax.axis_index("gx"), lax.axis_index("gy")
    has = lambda c: jnp.where(c, 1.0, 0.0).astype(jnp.float32)
    has_top, has_bottom = has(gx > 0), has(gx < ngx - 1)
    has_west, has_east = has(gy > 0), has(gy < ngy - 1)

    lane = lanes((lev, cy))
    eye = lane == lax.broadcasted_iota(jnp.int32, (lev, cy), 0)

    def corner(msg, i, flag):
        row = msg[cx + 1 + i : cx + 2 + i, :]
        return flag * jnp.sum(jnp.where(eye, row, 0.0), axis=1, keepdims=True)

    corners = [
        (corner(west, i, flag * has_west), corner(east, i, flag * has_east))
        for i, flag in enumerate((has_top, has_bottom))
    ]
    for msg, mine, flag, i in ((top, up, has_top, 0), (bottom, down, has_bottom, 1)):
        near = msg[0:lev, :] * flag
        far = msg[lev : 2 * lev, :] * flag
        w_corner, e_corner = corners[i]
        side = pltpu.roll(jnp.where(lane == cy - 1, w_corner, near), 1, 1) + pltpu.roll(
            jnp.where(lane == 0, e_corner, near), cy - 1, 1
        )
        gain = msg[2 * lev : 2 * lev + 1, :] * (horiz * flag)
        outer = (
            centre * near
            + gain * (side + far + mine[...])
            + vert * (shifted(near, 1, 0) + shifted(near, -1, 0))
        )
        ring[i * lev : (i + 1) * lev, :] = outer

    lane = lanes((cx, cy))
    odd = lane % 2 == 1
    west_cols = west[0:cx, :] * has_west
    east_cols = east[0:cx, :] * has_east
    w_gain = jnp.transpose(jnp.broadcast_to(west[cx : cx + 1, :], (cx, cx))) * (horiz * has_west)
    e_gain = jnp.transpose(jnp.broadcast_to(east[cx : cx + 1, :], (cx, cx))) * (horiz * has_east)
    merged = jnp.where(odd, west_cols, east_cols)
    given = merged * (horiz * jnp.where(odd, wet[:, 0:1], wet[:, cy - 1 : cy]))
    ring[2 * lev : 2 * lev + cx, :] = pltpu.roll(
        jnp.where(odd, given, pltpu.roll(given, cy - 2, 1)), cy - 1, 1
    )
    beside = (
        jnp.where(odd, pltpu.roll(west_cols, 1, 1), pltpu.roll(east_cols, cy - 1, 1))
        + jnp.where(odd, pltpu.roll(left[0:cx, :], cy - 1, 1), pltpu.roll(right[0:cx, :], 1, 1))
    )
    offset = lane[0:lev, :] - 2 * lax.broadcasted_iota(jnp.int32, (lev, cy), 0)
    at_west, at_east = offset == 1, (offset == 2) | (offset == 2 - cy)
    beyond = [
        jnp.sum(jnp.where(at_west, w, 0.0) + jnp.where(at_east, e, 0.0), axis=0, keepdims=True)
        for w, e in corners
    ]
    sub = lax.broadcasted_iota(jnp.int32, (cx, cy), 0)
    above = jnp.where(sub == 0, beyond[0], pltpu.roll(merged, 1, 0))
    below = jnp.where(sub == cx - 1, beyond[1], pltpu.roll(merged, cx - 1, 0))
    less = jnp.where((lane == 1) | (lane == 2), 0.0, pltpu.roll(merged, 2, 1))
    more = jnp.where((lane == cy - 1) | (lane == 0), 0.0, pltpu.roll(merged, cy - 2, 1))
    merged = (
        centre * merged
        + jnp.where(odd, w_gain, e_gain) * (beside + above + below)
        + vert * (less + more)
    )
    ring[2 * lev + cx :, :] = pltpu.roll(jnp.where(odd, merged, pltpu.roll(merged, cy - 2, 1)), cy - 1, 1)


def outer_ring(own, top, bottom, west, east, ngx, ngy):
    cx, cy = west.shape[0] - 8, west.shape[1]
    lev = top.shape[0] // 2 - 4
    return pl.pallas_call(
        functools.partial(ring_kernel, ngx, ngy),
        out_shape=jax.ShapeDtypeStruct((2 * lev + 2 * cx, cy), jnp.float32),
        in_specs=[VMEM] * 5,
        out_specs=VMEM,
        compiler_params=params(8),
        cost_estimate=pl.CostEstimate(flops=10**6, bytes_accessed=10**5, transcendentals=0),
    )(own, top, bottom, west, east)


def step_kernel(ngx, group, second, own, x, *refs):
    if second:
        ring, out, surface, hwet, buf, res, osems = refs
    else:
        top, bottom, res, hwet, buf = refs
    lev, cx, cy = x.shape
    pieces = lev // group

    def leave(i):
        part = pl.ds(i * group, group)
        return pltpu.make_async_copy(res.at[part], out.at[part], osems.at[i])

    ocean = lax.axis_index("mp") == 1
    horiz = jnp.where(ocean, HORIZ[1], HORIZ[0]).astype(jnp.float32)
    vert = jnp.where(ocean, VERT[1], VERT[0]).astype(jnp.float32)
    centre = 1.0 - 4.0 * horiz - 2.0 * vert
    wet = own.at[pl.ds(0, cx)]
    hwet[...] = wet[...] * horiz
    lane = lanes((cx, cy))
    ends = (lane == 0) | (lane == cy - 1)
    height = cx + 2 * PAD
    flat = buf.reshape((lev + 2) * height, cy)
    above, below = pl.ds(height + PAD - 1, lev, stride=height), pl.ds(height + PAD + cx, lev, stride=height)
    if second:
        flat[above, :] = ring[0:lev, :]
        flat[below, :] = ring[lev : 2 * lev, :]
    else:
        gx = lax.axis_index("gx")
        flat[above, :] = top[0:lev, :] * jnp.where(gx > 0, 1.0, 0.0).astype(jnp.float32)
        flat[below, :] = bottom[0:lev, :] * jnp.where(gx < ngx - 1, 1.0, 0.0).astype(jnp.float32)
    buf[0] = jnp.zeros((height, cy), jnp.float32)
    buf[lev + 1] = jnp.zeros((height, cy), jnp.float32)

    apart = lax.broadcasted_iota(jnp.int32, (cy, cy), 0) - lanes((cy, cy))
    pairs = jnp.where((apart == 1) | (apart == -1), 1.0, 0.0).astype(jnp.bfloat16)
    pairs = jnp.concatenate([pairs, pairs], axis=0)

    def beside_of(here):
        high = here.astype(jnp.bfloat16)
        low = (here - high.astype(jnp.float32)).astype(jnp.bfloat16)
        both = jnp.concatenate([high, low], axis=1)
        return jnp.dot(both, pairs, preferred_element_type=jnp.float32)

    def columns(part, start):
        off = 2 * lev + part * cx
        return pltpu.roll(ring[off : off + cx, :], lax.rem(2 * cy - 2 * start, cy), 1)

    def at_ends(sides, j):
        return jnp.where(ends, pltpu.roll(sides, (cy - 2 * j) % cy, 1), 0.0)

    def accept(i):
        sides = columns(0, i * group) if second else None
        for j in range(group):
            here = x[i * group + j]
            here = here + at_ends(sides, j) if second else here * wet[...]
            buf[i * group + j + 1, PAD : PAD + cx, :] = here

    def levels(start, count):
        sides = columns(1, start) if second else None
        for j in range(count):
            l = start + j
            here = buf[l + 1, PAD : PAD + cx, :]
            around = (
                beside_of(here)
                + buf[l + 1, PAD - 1 : PAD - 1 + cx, :]
                + buf[l + 1, PAD + 1 : PAD + 1 + cx, :]
            )
            if second:
                around = around + at_ends(sides, j)
            column = buf[l, PAD : PAD + cx, :] + buf[l + 2, PAD : PAD + cx, :]
            res[l] = centre * here + hwet[...] * around + vert * column

    accept(0)
    levels(0, group - 1)
    if second:
        surface[...] = res[0]

    def middle(i, _):
        accept(i)
        levels(i * group - 1, group)
        if second:
            leave(i - 1).start()
        return 0

    lax.fori_loop(1, pieces, middle, 0)
    levels(lev - 1, 1)
    if second:
        leave(pieces - 1).start()
        for i in range(pieces):
            leave(i).wait()


def one_step(own, x, outside, ngx, second):
    lev, cx, cy = x.shape
    group = 8
    whole = jax.ShapeDtypeStruct(x.shape, jnp.float32)
    return pl.pallas_call(
        functools.partial(step_kernel, ngx, group, second),
        out_shape=(whole, jax.ShapeDtypeStruct((cx, cy), jnp.float32)) if second else whole,
        in_specs=[VMEM] * (2 + len(outside)),
        out_specs=(ANY, VMEM) if second else VMEM,
        scratch_shapes=[
            pltpu.VMEM((cx, cy), jnp.float32),
            pltpu.VMEM((lev + 2, cx + 2 * PAD, cy), jnp.float32),
        ]
        + [pltpu.VMEM(x.shape, jnp.float32), pltpu.SemaphoreType.DMA((lev // group,))] * second,
        compiler_params=params(16),
        cost_estimate=pl.CostEstimate(
            flops=10**6 if second else FIRST_COST, bytes_accessed=10**5, transcendentals=0
        ),
    )(own, x, *outside)


def collect_kernel(ndev, own, got, surface, second, out, received, level, onehot, sums, sems, rsems):
    block = got.shape[0] // ndev
    extra = block - 8 * CAP
    fields, cx, cy = received.shape
    slots = ndev * CAP
    store = pltpu.make_async_copy(level, out.at[0], sems.at[0])

    def leave(i):
        part = pl.ds(i * fields // 2, fields // 2)
        return pltpu.make_async_copy(sums.at[part], received.at[part], rsems.at[i])

    labels = got[block - extra : block, :]
    for s in range(1, ndev):
        labels = labels + got[(s + 1) * block - extra : (s + 1) * block, :]
    labels = labels.astype(jnp.int32)
    want = lax.broadcasted_iota(jnp.int32, (cx, 128), 0) + 1
    wide = jnp.concatenate([labels[q : q + 1, :] == want for q in range(slots // 128)], axis=1)
    hot = jnp.where(wide, 1.0, 0.0).astype(jnp.bfloat16)
    onehot[:, 0:slots] = hot
    onehot[:, slots:] = hot
    for k in range(fields):
        x = jnp.concatenate([got[pl.ds(s * block + k, CAP, stride=8), :] for s in range(ndev)], axis=0)
        high = x.astype(jnp.bfloat16)
        low = (x - high.astype(jnp.float32)).astype(jnp.bfloat16)
        sums[k] = jnp.dot(
            onehot[...], jnp.concatenate([high, low], axis=0), preferred_element_type=jnp.float32
        )
        if k == fields // 2 - 1:
            leave(0).start()
        if k == 0:
            level[...] = surface[...] + FORCE * own[0:cx, :] * sums[0]
            store.start()
    leave(1).start()
    store.wait()
    leave(0).wait()
    leave(1).wait()


def collect(own, got, surface, second, fields, ndev):
    _, cx, cy = second.shape
    return pl.pallas_call(
        functools.partial(collect_kernel, ndev),
        out_shape=(
            jax.ShapeDtypeStruct(second.shape, jnp.float32),
            jax.ShapeDtypeStruct((fields, cx, cy), jnp.float32),
        ),
        in_specs=[VMEM, VMEM, VMEM, ANY],
        out_specs=(ANY, ANY),
        scratch_shapes=[
            pltpu.VMEM((cx, cy), jnp.float32),
            pltpu.VMEM((cx, 2 * ndev * CAP), jnp.bfloat16),
            pltpu.VMEM((fields, cx, cy), jnp.float32),
            pltpu.SemaphoreType.DMA((1,)),
            pltpu.SemaphoreType.DMA((2,)),
        ],
        input_output_aliases={3: 0},
        compiler_params=params(16),
        cost_estimate=pl.CostEstimate(flops=10**8, bytes_accessed=2 * 10**6, transcendentals=0),
    )(own, got, surface, second)


def local(states, surface, land_mask, tile_weights, tile_source, tile_target, tile_row):
    ngx, ngy = lax.axis_size("gx"), lax.axis_size("gy")
    ndev = ngx * ngy
    state, fields = states[0], surface.shape[1]
    cx, cy = land_mask.shape
    ahead = lambda n: [(i, (i + 1) % n) for i in range(n)]
    behind = lambda n: [((i + 1) % n, i) for i in range(n)]
    buckets, up, down, own = outgoing(
        tile_source[0, 0, 0],
        tile_target[0, 0, 0, :, 0],
        tile_row[0, 0, 0],
        land_mask,
        surface.reshape(fields * cx, cy),
        tile_weights[0, 0, 0],
        state,
        ngx,
        ngy,
    )
    top = lax.ppermute(down, "gx", ahead(ngx))
    bottom = lax.ppermute(up, "gx", behind(ngx))
    buckets = lax.ppermute(buckets, "mp", [(0, 1), (1, 0)])
    whole = buckets.shape
    buckets = buckets.reshape(ndev, whole[0] // ndev, 1, whole[1])
    got = lax.all_to_all(buckets, ("gx", "gy"), split_axis=0, concat_axis=0, tiled=True)
    got = got.reshape(whole)
    to_west, to_east = relay(own, top, bottom, cx)
    west = lax.ppermute(to_east, "gy", ahead(ngy))
    east = lax.ppermute(to_west, "gy", behind(ngy))
    first = one_step(own, state, (top, bottom), ngx, False)
    ring = outer_ring(own, top, bottom, west, east, ngx, ngy)
    second, level = one_step(own, first, (ring,), ngx, True)
    new_state, received = collect(own, got, level, second, fields, ndev)
    return new_state[None], received[None]


def solution(mesh):
    return jax.shard_map(
        local,
        mesh=mesh,
        in_specs=(
            P("mp", None, "gx", "gy"),
            P("mp", None, "gx", "gy"),
            P("gx", "gy"),
            P("mp", "gx", "gy", None, None, None),
            P("mp", "gx", "gy", None),
            P("mp", "gx", "gy", None, None),
            P("mp", "gx", "gy", None),
        ),
        out_specs=(P("mp", None, "gx", "gy"), P("mp", None, "gx", "gy")),
        check_vma=False,
    )
```

```python
import functools

import jax
import jax.numpy as jnp
from jax import lax
from jax.experimental import pallas as pl
from jax.experimental.pallas import tpu as pltpu
from jax.sharding import PartitionSpec as P

CAP = 8
FORCE = 0.5
HORIZ = (0.15, 0.12)
VERT = (0.1, 0.15)
MIB = 1024 * 1024
LIMIT = 60
FIRST_COST = 5 * 10**9
ANY = pl.BlockSpec(memory_space=pl.ANY)
VMEM = pl.BlockSpec(memory_space=pltpu.VMEM)
SMEM = pl.BlockSpec(memory_space=pltpu.SMEM)


def params(mib):
    return pltpu.CompilerParams(vmem_limit_bytes=mib * MIB)


def wet_of(mask_ref):
    ocean = lax.axis_index("mp") == 1
    return jnp.where(ocean, mask_ref[...].astype(jnp.float32), 1.0)


def lanes(shape):
    return lax.broadcasted_iota(jnp.int32, shape, len(shape) - 1)


def parts(lev, cx):
    sizes, start, out = (cx, lev, lev, cx + 8, cx + 8), 0, []
    for size in sizes:
        out.append(pl.ds(start, size))
        start += size
    return out


def send_kernel(
    ndev, ngy, chunk, group, tile_source, tile_target, tile_row, mask, surface, weights, state,
    out, up, down, own,
    src, tgt, row, count, labels, mbuf, sbuf, wbuf, buf, sems, wsems, usems,
):
    lev, cx, cy = state.shape
    tiles, band = weights.shape[0], 64
    wet, up_near, down_near, left, right = (own.at[part] for part in parts(lev, cx))
    held = sbuf.at[pl.ds(0, surface.shape[0])]
    small = [
        pltpu.make_async_copy(a, b, sems.at[i])
        for i, (a, b) in enumerate(
            ((tile_source, src), (tile_target, tgt), (tile_row, row), (mask, mbuf), (surface, held))
        )
    ]
    for copy in small:
        copy.start()
    wcopies, ucopies = [], []
    for i in range(tiles // chunk):
        part = pl.ds(i * chunk, chunk)
        wcopies.append(pltpu.make_async_copy(weights.at[part], wbuf.at[part], wsems.at[i]))
        wcopies[-1].start()
    for i in range(cx // band):
        part = (slice(None), pl.ds(i * band, band), slice(None))
        ucopies.append(pltpu.make_async_copy(state.at[part], buf.at[part], usems.at[i]))
        ucopies[-1].start()
    block = out.shape[0] // ndev
    extra = block - 8 * CAP
    out[...] = jnp.zeros_like(out)
    labels[...] = jnp.zeros_like(labels)
    for d in range(ndev):
        count[d] = 0
    me = lax.axis_index("gx") * ngy + lax.axis_index("gy")
    place = lax.broadcasted_iota(jnp.int32, (8, 128), 0) * 128 + lanes((8, 128))
    for copy in small:
        copy.wait()
    wet[...] = wet_of(mbuf)

    per = 128 // 8
    own_lanes = lanes((cy, 128)) // 8

    def some(start):
        picked = []
        for t in range(start, start + per):
            s = src[t]
            picked.append(sbuf[pl.ds(s, 8, stride=cx), :] * wet[pl.ds(s, 1), :])
        rounded = jnp.concatenate(picked, axis=0).astype(jnp.bfloat16).astype(jnp.float32)
        turned = jnp.transpose(rounded)
        apart = [jnp.where(own_lanes == i, turned, 0.0).astype(jnp.bfloat16) for i in range(per)]
        total = jnp.dot(
            jnp.concatenate([wbuf[start + i] for i in range(per)], axis=1),
            jnp.concatenate(apart, axis=0),
            preferred_element_type=jnp.float32,
        )
        total = jnp.transpose(total)
        for i in range(per):
            t = start + i
            d = tgt[t]
            rank = count[d]
            count[d] = rank + 1
            out[pl.ds(d * block + rank * 8, 8), :] = total[i * 8 : (i + 1) * 8, :]
            label = (row[t] + 1).astype(jnp.float32)
            labels[d] = jnp.where(place == me * CAP + rank, label, labels[d])

    for i in range(tiles // chunk):
        wcopies[i].wait()
        for start in range(i * chunk, (i + 1) * chunk, per):
            some(start)
    for d in range(ndev):
        out[(d + 1) * block - extra : (d + 1) * block, :] = labels[d, 0:extra, :]

    turned = jnp.transpose(wet[...])
    up[2 * lev :, :] = jnp.broadcast_to(wet[0:1, :], (8, cy))
    down[2 * lev :, :] = jnp.broadcast_to(wet[cx - 1 :, :], (8, cy))
    left[cx:, :] = jnp.broadcast_to(turned[0:1, :], (8, cx))
    right[cx:, :] = jnp.broadcast_to(turned[cy - 1 :, :], (8, cx))
    strip = 32
    flat = buf.reshape(lev * cx, cy)
    lane = lanes((strip, cy))
    even, low_half = lane % 2 == 0, lane % 4 < 2
    fours = lane // 4, lax.rem(lane + cy - 2, cy) // 4
    for i in range(cx // band):
        ucopies[i].wait()
        for b in range(i * band // strip, (i + 1) * band // strip):
            rows = pl.ds(b * strip, strip)
            gathered = [jnp.zeros((strip, cy), jnp.float32)] * 2
            for l in range(lev):
                moved = pltpu.roll(buf[l, rows, :], (2 * l + 2) % cy, 1)
                gathered[l % 2] = jnp.where(fours[l % 2] == l // 2, moved, gathered[l % 2])
            edge = wet[rows, :]
            lo = jnp.where(low_half, gathered[1], gathered[0])
            hi = jnp.where(low_half, gathered[0], gathered[1])
            left[rows, :] = lo * jnp.where(even, edge[:, 0:1], edge[:, 1:2])
            right[rows, :] = hi * jnp.where(even, edge[:, cy - 2 : cy - 1], edge[:, cy - 1 :])
    for dst, off, r in ((up, 0, 0), (up, lev, 1), (down, 0, cx - 1), (down, lev, cx - 2)):
        dst[off : off + lev, :] = flat[pl.ds(r, lev, stride=cx), :] * wet[r : r + 1, :]
    up_near[...] = up[0:lev, :]
    down_near[...] = down[0:lev, :]


def outgoing(tile_source, tile_target, tile_row, mask, surface, weights, state, ngx, ngy):
    tiles = weights.shape[0]
    lev, cx, cy = state.shape
    ndev, chunk, group = ngx * ngy, 32, lev
    block = 8 * CAP + ndev * CAP // 128
    message = jax.ShapeDtypeStruct((2 * lev + 8, cy), jnp.float32)
    return pl.pallas_call(
        functools.partial(send_kernel, ndev, ngy, chunk, group),
        out_shape=(
            jax.ShapeDtypeStruct((ndev * block, 128), jnp.float32),
            message,
            message,
            jax.ShapeDtypeStruct((parts(lev, cx)[-1].start + cx + 8, cy), jnp.float32),
        ),
        in_specs=[ANY] * 7,
        out_specs=(VMEM,) * 4,
        scratch_shapes=[
            pltpu.SMEM((tiles,), jnp.int32),
            pltpu.SMEM((tiles,), jnp.int32),
            pltpu.SMEM((tiles,), jnp.int32),
            pltpu.SMEM((ndev,), jnp.int32),
            pltpu.VMEM((ndev, 8, 128), jnp.float32),
            pltpu.VMEM(mask.shape, jnp.int32),
            pltpu.VMEM((surface.shape[0] + cx, cy), jnp.float32),
            pltpu.VMEM(weights.shape, weights.dtype),
            pltpu.VMEM(state.shape, jnp.float32),
            pltpu.SemaphoreType.DMA((5,)),
            pltpu.SemaphoreType.DMA((tiles // chunk,)),
            pltpu.SemaphoreType.DMA((4,)),
        ],
        compiler_params=params(16),
        cost_estimate=pl.CostEstimate(flops=10**8, bytes_accessed=8 * 10**6, transcendentals=0),
    )(
        *[
            pltpu.with_memory_space_constraint(x, pltpu.HBM)
            for x in (tile_source, tile_target, tile_row, mask, surface, weights, state)
        ]
    )


def shifted(x, by, axis):
    size = x.shape[axis]
    moved = pltpu.roll(x, by % size, axis)
    index = lax.broadcasted_iota(jnp.int32, x.shape, axis)
    return jnp.where(index == (0 if by == 1 else size - 1), 0.0, moved)


PAD = 8


def relay_kernel(own, top, bottom, to_west, to_east):
    cx = to_west.shape[0] - 8
    cy = to_west.shape[1]
    lev = top.shape[0] // 2 - 4
    eye = lanes((lev, cy)) == lax.broadcasted_iota(jnp.int32, (lev, cy), 0)
    for out, part, c in ((to_west, parts(lev, cx)[3], 0), (to_east, parts(lev, cx)[4], cy - 1)):
        out[...] = own[part, :]
        for i, msg in enumerate((top, bottom)):
            column = msg[0:lev, c : c + 1]
            row = jnp.sum(jnp.where(eye, column, 0.0), axis=0, keepdims=True)
            out[cx + 1 + i : cx + 2 + i, :] = row


def relay(own, top, bottom, cx):
    cy = own.shape[1]
    columns = jax.ShapeDtypeStruct((cx + 8, cy), jnp.float32)
    return pl.pallas_call(
        relay_kernel,
        out_shape=(columns, columns),
        in_specs=[VMEM] * 3,
        out_specs=(VMEM, VMEM),
        compiler_params=params(8),
        cost_estimate=pl.CostEstimate(flops=10**11, bytes_accessed=10**8, transcendentals=0),
    )(own, top, bottom)


def ring_kernel(ngx, ngy, own, top, bottom, west, east, ring):
    cx, cy = west.shape[0] - 8, west.shape[1]
    lev = top.shape[0] // 2 - 4
    wet, up, down, left, right = (own.at[part] for part in parts(lev, cx))
    ocean = lax.axis_index("mp") == 1
    horiz = jnp.where(ocean, HORIZ[1], HORIZ[0]).astype(jnp.float32)
    vert = jnp.where(ocean, VERT[1], VERT[0]).astype(jnp.float32)
    centre = 1.0 - 4.0 * horiz - 2.0 * vert
    gx, gy = lax.axis_index("gx"), lax.axis_index("gy")
    has = lambda c: jnp.where(c, 1.0, 0.0).astype(jnp.float32)
    has_top, has_bottom = has(gx > 0), has(gx < ngx - 1)
    has_west, has_east = has(gy > 0), has(gy < ngy - 1)

    lane = lanes((lev, cy))
    eye = lane == lax.broadcasted_iota(jnp.int32, (lev, cy), 0)

    def corner(msg, i, flag):
        row = msg[cx + 1 + i : cx + 2 + i, :]
        return flag * jnp.sum(jnp.where(eye, row, 0.0), axis=1, keepdims=True)

    corners = [
        (corner(west, i, flag * has_west), corner(east, i, flag * has_east))
        for i, flag in enumerate((has_top, has_bottom))
    ]
    for msg, mine, flag, i in ((top, up, has_top, 0), (bottom, down, has_bottom, 1)):
        near = msg[0:lev, :] * flag
        far = msg[lev : 2 * lev, :] * flag
        w_corner, e_corner = corners[i]
        side = pltpu.roll(jnp.where(lane == cy - 1, w_corner, near), 1, 1) + pltpu.roll(
            jnp.where(lane == 0, e_corner, near), cy - 1, 1
        )
        gain = msg[2 * lev : 2 * lev + 1, :] * (horiz * flag)
        outer = (
            centre * near
            + gain * (side + far + mine[...])
            + vert * (shifted(near, 1, 0) + shifted(near, -1, 0))
        )
        ring[i * lev : (i + 1) * lev, :] = outer

    lane = lanes((cx, cy))
    odd = lane % 2 == 1
    west_cols = west[0:cx, :] * has_west
    east_cols = east[0:cx, :] * has_east
    w_gain = jnp.transpose(jnp.broadcast_to(west[cx : cx + 1, :], (cx, cx))) * (horiz * has_west)
    e_gain = jnp.transpose(jnp.broadcast_to(east[cx : cx + 1, :], (cx, cx))) * (horiz * has_east)
    merged = jnp.where(odd, west_cols, east_cols)
    given = merged * (horiz * jnp.where(odd, wet[:, 0:1], wet[:, cy - 1 : cy]))
    ring[2 * lev : 2 * lev + cx, :] = pltpu.roll(
        jnp.where(odd, given, pltpu.roll(given, cy - 2, 1)), cy - 1, 1
    )
    beside = (
        jnp.where(odd, pltpu.roll(west_cols, 1, 1), pltpu.roll(east_cols, cy - 1, 1))
        + jnp.where(odd, pltpu.roll(left[0:cx, :], cy - 1, 1), pltpu.roll(right[0:cx, :], 1, 1))
    )
    offset = lane[0:lev, :] - 2 * lax.broadcasted_iota(jnp.int32, (lev, cy), 0)
    at_west, at_east = offset == 1, (offset == 2) | (offset == 2 - cy)
    beyond = [
        jnp.sum(jnp.where(at_west, w, 0.0) + jnp.where(at_east, e, 0.0), axis=0, keepdims=True)
        for w, e in corners
    ]
    sub = lax.broadcasted_iota(jnp.int32, (cx, cy), 0)
    above = jnp.where(sub == 0, beyond[0], pltpu.roll(merged, 1, 0))
    below = jnp.where(sub == cx - 1, beyond[1], pltpu.roll(merged, cx - 1, 0))
    less = jnp.where((lane == 1) | (lane == 2), 0.0, pltpu.roll(merged, 2, 1))
    more = jnp.where((lane == cy - 1) | (lane == 0), 0.0, pltpu.roll(merged, cy - 2, 1))
    merged = (
        centre * merged
        + jnp.where(odd, w_gain, e_gain) * (beside + above + below)
        + vert * (less + more)
    )
    ring[2 * lev + cx :, :] = pltpu.roll(jnp.where(odd, merged, pltpu.roll(merged, cy - 2, 1)), cy - 1, 1)


def outer_ring(own, top, bottom, west, east, ngx, ngy):
    cx, cy = west.shape[0] - 8, west.shape[1]
    lev = top.shape[0] // 2 - 4
    return pl.pallas_call(
        functools.partial(ring_kernel, ngx, ngy),
        out_shape=jax.ShapeDtypeStruct((2 * lev + 2 * cx, cy), jnp.float32),
        in_specs=[VMEM] * 5,
        out_specs=VMEM,
        compiler_params=params(8),
        cost_estimate=pl.CostEstimate(flops=10**6, bytes_accessed=10**5, transcendentals=0),
    )(own, top, bottom, west, east)


def step_kernel(ngx, group, second, own, x, *refs):
    if second:
        ring, out, surface, hwet, buf, res, osems = refs
    else:
        top, bottom, res, hwet, buf = refs
    lev, cx, cy = x.shape
    pieces = lev // group

    def leave(i):
        part = pl.ds(i * group, group)
        return pltpu.make_async_copy(res.at[part], out.at[part], osems.at[i])

    ocean = lax.axis_index("mp") == 1
    horiz = jnp.where(ocean, HORIZ[1], HORIZ[0]).astype(jnp.float32)
    vert = jnp.where(ocean, VERT[1], VERT[0]).astype(jnp.float32)
    centre = 1.0 - 4.0 * horiz - 2.0 * vert
    wet = own.at[pl.ds(0, cx)]
    hwet[...] = wet[...] * horiz
    lane = lanes((cx, cy))
    ends = (lane == 0) | (lane == cy - 1)
    height = cx + 2 * PAD
    flat = buf.reshape((lev + 2) * height, cy)
    above, below = pl.ds(height + PAD - 1, lev, stride=height), pl.ds(height + PAD + cx, lev, stride=height)
    if second:
        flat[above, :] = ring[0:lev, :]
        flat[below, :] = ring[lev : 2 * lev, :]
    else:
        gx = lax.axis_index("gx")
        flat[above, :] = top[0:lev, :] * jnp.where(gx > 0, 1.0, 0.0).astype(jnp.float32)
        flat[below, :] = bottom[0:lev, :] * jnp.where(gx < ngx - 1, 1.0, 0.0).astype(jnp.float32)
    buf[0] = jnp.zeros((height, cy), jnp.float32)
    buf[lev + 1] = jnp.zeros((height, cy), jnp.float32)

    apart = lax.broadcasted_iota(jnp.int32, (cy, cy), 0) - lanes((cy, cy))
    pairs = jnp.where((apart == 1) | (apart == -1), 1.0, 0.0).astype(jnp.bfloat16)
    pairs = jnp.concatenate([pairs, pairs], axis=0)

    def beside_of(here):
        high = here.astype(jnp.bfloat16)
        low = (here - high.astype(jnp.float32)).astype(jnp.bfloat16)
        both = jnp.concatenate([high, low], axis=1)
        return jnp.dot(both, pairs, preferred_element_type=jnp.float32)

    def columns(part, start):
        off = 2 * lev + part * cx
        return pltpu.roll(ring[off : off + cx, :], lax.rem(2 * cy - 2 * start, cy), 1)

    def at_ends(sides, j):
        return jnp.where(ends, pltpu.roll(sides, (cy - 2 * j) % cy, 1), 0.0)

    def accept(i):
        sides = columns(0, i * group) if second else None
        for j in range(group):
            here = x[i * group + j]
            here = here + at_ends(sides, j) if second else here * wet[...]
            buf[i * group + j + 1, PAD : PAD + cx, :] = here

    def levels(start, count):
        sides = columns(1, start) if second else None
        for j in range(count):
            l = start + j
            here = buf[l + 1, PAD : PAD + cx, :]
            around = (
                beside_of(here)
                + buf[l + 1, PAD - 1 : PAD - 1 + cx, :]
                + buf[l + 1, PAD + 1 : PAD + 1 + cx, :]
            )
            if second:
                around = around + at_ends(sides, j)
            column = buf[l, PAD : PAD + cx, :] + buf[l + 2, PAD : PAD + cx, :]
            res[l] = centre * here + hwet[...] * around + vert * column

    accept(0)
    levels(0, group - 1)
    if second:
        surface[...] = res[0]

    def middle(i, _):
        accept(i)
        levels(i * group - 1, group)
        if second:
            leave(i - 1).start()
        return 0

    lax.fori_loop(1, pieces, middle, 0)
    levels(lev - 1, 1)
    if second:
        leave(pieces - 1).start()
        for i in range(pieces):
            leave(i).wait()


def one_step(own, x, outside, ngx, second):
    lev, cx, cy = x.shape
    group = 8
    whole = jax.ShapeDtypeStruct(x.shape, jnp.float32)
    return pl.pallas_call(
        functools.partial(step_kernel, ngx, group, second),
        out_shape=(whole, jax.ShapeDtypeStruct((cx, cy), jnp.float32)) if second else whole,
        in_specs=[VMEM] * (2 + len(outside)),
        out_specs=(ANY, VMEM) if second else VMEM,
        scratch_shapes=[
            pltpu.VMEM((cx, cy), jnp.float32),
            pltpu.VMEM((lev + 2, cx + 2 * PAD, cy), jnp.float32),
        ]
        + [pltpu.VMEM(x.shape, jnp.float32), pltpu.SemaphoreType.DMA((lev // group,))] * second,
        compiler_params=params(16),
        cost_estimate=pl.CostEstimate(
            flops=10**6 if second else FIRST_COST, bytes_accessed=10**5, transcendentals=0
        ),
    )(own, x, *outside)


def collect_kernel(ndev, own, got, surface, second, out, received, level, onehot, sums, sems, rsems):
    block = got.shape[0] // ndev
    extra = block - 8 * CAP
    fields, cx, cy = received.shape
    slots = ndev * CAP
    store = pltpu.make_async_copy(level, out.at[0], sems.at[0])

    def leave(i):
        part = pl.ds(i * fields // 2, fields // 2)
        return pltpu.make_async_copy(sums.at[part], received.at[part], rsems.at[i])

    labels = got[block - extra : block, :]
    for s in range(1, ndev):
        labels = labels + got[(s + 1) * block - extra : (s + 1) * block, :]
    labels = labels.astype(jnp.int32)
    want = lax.broadcasted_iota(jnp.int32, (cx, 128), 0) + 1
    wide = jnp.concatenate([labels[q : q + 1, :] == want for q in range(slots // 128)], axis=1)
    hot = jnp.where(wide, 1.0, 0.0).astype(jnp.bfloat16)
    onehot[:, 0:slots] = hot
    onehot[:, slots:] = hot
    for k in range(fields):
        x = jnp.concatenate([got[pl.ds(s * block + k, CAP, stride=8), :] for s in range(ndev)], axis=0)
        high = x.astype(jnp.bfloat16)
        low = (x - high.astype(jnp.float32)).astype(jnp.bfloat16)
        sums[k] = jnp.dot(
            onehot[...], jnp.concatenate([high, low], axis=0), preferred_element_type=jnp.float32
        )
        if k == fields // 2 - 1:
            leave(0).start()
        if k == 0:
            level[...] = surface[...] + FORCE * own[0:cx, :] * sums[0]
            store.start()
    leave(1).start()
    store.wait()
    leave(0).wait()
    leave(1).wait()


def collect(own, got, surface, second, fields, ndev):
    _, cx, cy = second.shape
    return pl.pallas_call(
        functools.partial(collect_kernel, ndev),
        out_shape=(
            jax.ShapeDtypeStruct(second.shape, jnp.float32),
            jax.ShapeDtypeStruct((fields, cx, cy), jnp.float32),
        ),
        in_specs=[VMEM, VMEM, VMEM, ANY],
        out_specs=(ANY, ANY),
        scratch_shapes=[
            pltpu.VMEM((cx, cy), jnp.float32),
            pltpu.VMEM((cx, 2 * ndev * CAP), jnp.bfloat16),
            pltpu.VMEM((fields, cx, cy), jnp.float32),
            pltpu.SemaphoreType.DMA((1,)),
            pltpu.SemaphoreType.DMA((2,)),
        ],
        input_output_aliases={3: 0},
        compiler_params=params(16),
        cost_estimate=pl.CostEstimate(flops=10**8, bytes_accessed=2 * 10**6, transcendentals=0),
    )(own, got, surface, second)


def local(states, surface, land_mask, tile_weights, tile_source, tile_target, tile_row):
    ngx, ngy = lax.axis_size("gx"), lax.axis_size("gy")
    ndev = ngx * ngy
    state, fields = states[0], surface.shape[1]
    cx, cy = land_mask.shape
    ahead = lambda n: [(i, (i + 1) % n) for i in range(n)]
    behind = lambda n: [((i + 1) % n, i) for i in range(n)]
    buckets, up, down, own = outgoing(
        tile_source[0, 0, 0],
        tile_target[0, 0, 0, :, 0],
        tile_row[0, 0, 0],
        land_mask,
        surface.reshape(fields * cx, cy),
        tile_weights[0, 0, 0],
        state,
        ngx,
        ngy,
    )
    top = lax.ppermute(down, "gx", ahead(ngx))
    bottom = lax.ppermute(up, "gx", behind(ngx))
    buckets = lax.ppermute(buckets, "mp", [(0, 1), (1, 0)])
    whole = buckets.shape
    buckets = buckets.reshape(ndev, whole[0] // ndev, 1, whole[1])
    got = lax.all_to_all(buckets, ("gx", "gy"), split_axis=0, concat_axis=0, tiled=True)
    got = got.reshape(whole)
    to_west, to_east = relay(own, top, bottom, cx)
    west = lax.ppermute(to_east, "gy", ahead(ngy))
    east = lax.ppermute(to_west, "gy", behind(ngy))
    first = one_step(own, state, (top, bottom), ngx, False)
    ring = outer_ring(own, top, bottom, west, east, ngx, ngy)
    second, level = one_step(own, first, (ring,), ngx, True)
    new_state, received = collect(own, got, level, second, fields, ndev)
    return new_state[None], received[None]


def solution(mesh):
    return jax.shard_map(
        local,
        mesh=mesh,
        in_specs=(
            P("mp", None, "gx", "gy"),
            P("mp", None, "gx", "gy"),
            P("gx", "gy"),
            P("mp", "gx", "gy", None, None, None),
            P("mp", "gx", "gy", None),
            P("mp", "gx", "gy", None, None),
            P("mp", "gx", "gy", None),
        ),
        out_specs=(P("mp", None, "gx", "gy"), P("mp", None, "gx", "gy")),
        check_vma=False,
    )
```

```python
import functools

import jax
import jax.numpy as jnp
from jax import lax
from jax.experimental import pallas as pl
from jax.experimental.pallas import tpu as pltpu
from jax.sharding import PartitionSpec as P

CAP = 8
FORCE = 0.5
HORIZ = (0.15, 0.12)
VERT = (0.1, 0.15)
MIB = 1024 * 1024
LIMIT = 60
FIRST_COST = 5 * 10**9
ANY = pl.BlockSpec(memory_space=pl.ANY)
VMEM = pl.BlockSpec(memory_space=pltpu.VMEM)
SMEM = pl.BlockSpec(memory_space=pltpu.SMEM)


def params(mib):
    return pltpu.CompilerParams(vmem_limit_bytes=mib * MIB)


def wet_of(mask_ref):
    ocean = lax.axis_index("mp") == 1
    return jnp.where(ocean, mask_ref[...].astype(jnp.float32), 1.0)


def lanes(shape):
    return lax.broadcasted_iota(jnp.int32, shape, len(shape) - 1)


def parts(lev, cx):
    sizes, start, out = (cx, lev, lev, cx + 8, cx + 8), 0, []
    for size in sizes:
        out.append(pl.ds(start, size))
        start += size
    return out


def send_kernel(
    ndev, ngy, chunk, group, tile_source, tile_target, tile_row, mask, surface, weights, state,
    out, up, down, own,
    src, tgt, row, count, labels, mbuf, sbuf, wbuf, buf, sems, wsems, usems,
):
    lev, cx, cy = state.shape
    tiles, band = weights.shape[0], 64
    wet, up_near, down_near, left, right = (own.at[part] for part in parts(lev, cx))
    held = sbuf.at[pl.ds(0, surface.shape[0])]
    small = [
        pltpu.make_async_copy(a, b, sems.at[i])
        for i, (a, b) in enumerate(
            ((tile_source, src), (tile_target, tgt), (tile_row, row), (mask, mbuf), (surface, held))
        )
    ]
    for copy in small:
        copy.start()
    wcopies, ucopies = [], []
    for i in range(tiles // chunk):
        part = pl.ds(i * chunk, chunk)
        wcopies.append(pltpu.make_async_copy(weights.at[part], wbuf.at[part], wsems.at[i]))
        wcopies[-1].start()
    for i in range(cx // band):
        part = (slice(None), pl.ds(i * band, band), slice(None))
        ucopies.append(pltpu.make_async_copy(state.at[part], buf.at[part], usems.at[i]))
        ucopies[-1].start()
    block = out.shape[0] // ndev
    extra = block - 8 * CAP
    out[...] = jnp.zeros_like(out)
    labels[...] = jnp.zeros_like(labels)
    for d in range(ndev):
        count[d] = 0
    me = lax.axis_index("gx") * ngy + lax.axis_index("gy")
    place = lax.broadcasted_iota(jnp.int32, (8, 128), 0) * 128 + lanes((8, 128))
    for copy in small:
        copy.wait()
    wet[...] = wet_of(mbuf)

    per = 128 // 8
    own_lanes = lanes((cy, 128)) // 8

    def some(start):
        picked = []
        for t in range(start, start + per):
            s = src[t]
            picked.append(sbuf[pl.ds(s, 8, stride=cx), :] * wet[pl.ds(s, 1), :])
        rounded = jnp.concatenate(picked, axis=0).astype(jnp.bfloat16).astype(jnp.float32)
        turned = jnp.transpose(rounded)
        apart = [jnp.where(own_lanes == i, turned, 0.0).astype(jnp.bfloat16) for i in range(per)]
        total = jnp.dot(
            jnp.concatenate([wbuf[start + i] for i in range(per)], axis=1),
            jnp.concatenate(apart, axis=0),
            preferred_element_type=jnp.float32,
        )
        total = jnp.transpose(total)
        for i in range(per):
            t = start + i
            d = tgt[t]
            rank = count[d]
            count[d] = rank + 1
            out[pl.ds(d * block + rank * 8, 8), :] = total[i * 8 : (i + 1) * 8, :]
            label = (row[t] + 1).astype(jnp.float32)
            labels[d] = jnp.where(place == me * CAP + rank, label, labels[d])

    for i in range(tiles // chunk):
        wcopies[i].wait()
        for start in range(i * chunk, (i + 1) * chunk, per):
            some(start)
    for d in range(ndev):
        out[(d + 1) * block - extra : (d + 1) * block, :] = labels[d, 0:extra, :]

    turned = jnp.transpose(wet[...])
    up[2 * lev :, :] = jnp.broadcast_to(wet[0:1, :], (8, cy))
    down[2 * lev :, :] = jnp.broadcast_to(wet[cx - 1 :, :], (8, cy))
    left[cx:, :] = jnp.broadcast_to(turned[0:1, :], (8, cx))
    right[cx:, :] = jnp.broadcast_to(turned[cy - 1 :, :], (8, cx))
    strip = 32
    flat = buf.reshape(lev * cx, cy)
    lane = lanes((strip, cy))
    even, low_half = lane % 2 == 0, lane % 4 < 2
    fours = lane // 4, lax.rem(lane + cy - 2, cy) // 4
    for i in range(cx // band):
        ucopies[i].wait()
        for b in range(i * band // strip, (i + 1) * band // strip):
            rows = pl.ds(b * strip, strip)
            gathered = [jnp.zeros((strip, cy), jnp.float32)] * 2
            for l in range(lev):
                moved = pltpu.roll(buf[l, rows, :], (2 * l + 2) % cy, 1)
                gathered[l % 2] = jnp.where(fours[l % 2] == l // 2, moved, gathered[l % 2])
            edge = wet[rows, :]
            lo = jnp.where(low_half, gathered[1], gathered[0])
            hi = jnp.where(low_half, gathered[0], gathered[1])
            left[rows, :] = lo * jnp.where(even, edge[:, 0:1], edge[:, 1:2])
            right[rows, :] = hi * jnp.where(even, edge[:, cy - 2 : cy - 1], edge[:, cy - 1 :])
    for dst, off, r in ((up, 0, 0), (up, lev, 1), (down, 0, cx - 1), (down, lev, cx - 2)):
        dst[off : off + lev, :] = flat[pl.ds(r, lev, stride=cx), :] * wet[r : r + 1, :]
    up_near[...] = up[0:lev, :]
    down_near[...] = down[0:lev, :]


def outgoing(tile_source, tile_target, tile_row, mask, surface, weights, state, ngx, ngy):
    tiles = weights.shape[0]
    lev, cx, cy = state.shape
    ndev, chunk, group = ngx * ngy, 32, lev
    block = 8 * CAP + ndev * CAP // 128
    message = jax.ShapeDtypeStruct((2 * lev + 8, cy), jnp.float32)
    return pl.pallas_call(
        functools.partial(send_kernel, ndev, ngy, chunk, group),
        out_shape=(
            jax.ShapeDtypeStruct((ndev * block, 128), jnp.float32),
            message,
            message,
            jax.ShapeDtypeStruct((parts(lev, cx)[-1].start + cx + 8, cy), jnp.float32),
        ),
        in_specs=[ANY] * 7,
        out_specs=(VMEM,) * 4,
        scratch_shapes=[
            pltpu.SMEM((tiles,), jnp.int32),
            pltpu.SMEM((tiles,), jnp.int32),
            pltpu.SMEM((tiles,), jnp.int32),
            pltpu.SMEM((ndev,), jnp.int32),
            pltpu.VMEM((ndev, 8, 128), jnp.float32),
            pltpu.VMEM(mask.shape, jnp.int32),
            pltpu.VMEM((surface.shape[0] + cx, cy), jnp.float32),
            pltpu.VMEM(weights.shape, weights.dtype),
            pltpu.VMEM(state.shape, jnp.float32),
            pltpu.SemaphoreType.DMA((5,)),
            pltpu.SemaphoreType.DMA((tiles // chunk,)),
            pltpu.SemaphoreType.DMA((4,)),
        ],
        compiler_params=params(16),
        cost_estimate=pl.CostEstimate(flops=10**8, bytes_accessed=8 * 10**6, transcendentals=0),
    )(
        *[
            pltpu.with_memory_space_constraint(x, pltpu.HBM)
            for x in (tile_source, tile_target, tile_row, mask, surface, weights, state)
        ]
    )


def shifted(x, by, axis):
    size = x.shape[axis]
    moved = pltpu.roll(x, by % size, axis)
    index = lax.broadcasted_iota(jnp.int32, x.shape, axis)
    return jnp.where(index == (0 if by == 1 else size - 1), 0.0, moved)


PAD = 8


def relay_kernel(own, top, bottom, first, second):
    cx = first.shape[0] - 8
    cy = first.shape[1]
    lev = top.shape[0] // 2 - 4
    eye = lanes((lev, cy)) == lax.broadcasted_iota(jnp.int32, (lev, cy), 0)
    even = lax.rem(lax.axis_index("gy"), 2) == 0
    west, east = (own[part, :] for part in parts(lev, cx)[3:])
    first[...] = jnp.where(even, east, west)
    second[...] = jnp.where(even, west, east)
    for out, turn in ((first, even), (second, jnp.logical_not(even))):
        for i, msg in enumerate((top, bottom)):
            column = jnp.where(turn, msg[0:lev, cy - 1 : cy], msg[0:lev, 0:1])
            row = jnp.sum(jnp.where(eye, column, 0.0), axis=0, keepdims=True)
            out[cx + 1 + i : cx + 2 + i, :] = row


def relay(own, top, bottom, cx):
    cy = own.shape[1]
    columns = jax.ShapeDtypeStruct((cx + 8, cy), jnp.float32)
    return pl.pallas_call(
        relay_kernel,
        out_shape=(columns, columns),
        in_specs=[VMEM] * 3,
        out_specs=(VMEM, VMEM),
        compiler_params=params(8),
        cost_estimate=pl.CostEstimate(flops=10**11, bytes_accessed=10**8, transcendentals=0),
    )(own, top, bottom)


def ring_kernel(ngx, ngy, own, top, bottom, got_a, got_b, ring):
    cx, cy = got_a.shape[0] - 8, got_a.shape[1]
    even = lax.rem(lax.axis_index("gy"), 2) == 0
    a, b = got_a[...], got_b[...]
    west, east = jnp.where(even, b, a), jnp.where(even, a, b)
    lev = top.shape[0] // 2 - 4
    wet, up, down, left, right = (own.at[part] for part in parts(lev, cx))
    ocean = lax.axis_index("mp") == 1
    horiz = jnp.where(ocean, HORIZ[1], HORIZ[0]).astype(jnp.float32)
    vert = jnp.where(ocean, VERT[1], VERT[0]).astype(jnp.float32)
    centre = 1.0 - 4.0 * horiz - 2.0 * vert
    gx, gy = lax.axis_index("gx"), lax.axis_index("gy")
    has = lambda c: jnp.where(c, 1.0, 0.0).astype(jnp.float32)
    has_top, has_bottom = has(gx > 0), has(gx < ngx - 1)
    has_west, has_east = has(gy > 0), has(gy < ngy - 1)

    lane = lanes((lev, cy))
    eye = lane == lax.broadcasted_iota(jnp.int32, (lev, cy), 0)

    def corner(msg, i, flag):
        row = msg[cx + 1 + i : cx + 2 + i, :]
        return flag * jnp.sum(jnp.where(eye, row, 0.0), axis=1, keepdims=True)

    corners = [
        (corner(west, i, flag * has_west), corner(east, i, flag * has_east))
        for i, flag in enumerate((has_top, has_bottom))
    ]
    for msg, mine, flag, i in ((top, up, has_top, 0), (bottom, down, has_bottom, 1)):
        near = msg[0:lev, :] * flag
        far = msg[lev : 2 * lev, :] * flag
        w_corner, e_corner = corners[i]
        side = pltpu.roll(jnp.where(lane == cy - 1, w_corner, near), 1, 1) + pltpu.roll(
            jnp.where(lane == 0, e_corner, near), cy - 1, 1
        )
        gain = msg[2 * lev : 2 * lev + 1, :] * (horiz * flag)
        outer = (
            centre * near
            + gain * (side + far + mine[...])
            + vert * (shifted(near, 1, 0) + shifted(near, -1, 0))
        )
        ring[i * lev : (i + 1) * lev, :] = outer

    lane = lanes((cx, cy))
    odd = lane % 2 == 1
    west_cols = west[0:cx, :] * has_west
    east_cols = east[0:cx, :] * has_east
    w_gain = jnp.transpose(jnp.broadcast_to(west[cx : cx + 1, :], (cx, cx))) * (horiz * has_west)
    e_gain = jnp.transpose(jnp.broadcast_to(east[cx : cx + 1, :], (cx, cx))) * (horiz * has_east)
    merged = jnp.where(odd, west_cols, east_cols)
    given = merged * (horiz * jnp.where(odd, wet[:, 0:1], wet[:, cy - 1 : cy]))
    ring[2 * lev : 2 * lev + cx, :] = pltpu.roll(
        jnp.where(odd, given, pltpu.roll(given, cy - 2, 1)), cy - 1, 1
    )
    beside = (
        jnp.where(odd, pltpu.roll(west_cols, 1, 1), pltpu.roll(east_cols, cy - 1, 1))
        + jnp.where(odd, pltpu.roll(left[0:cx, :], cy - 1, 1), pltpu.roll(right[0:cx, :], 1, 1))
    )
    offset = lane[0:lev, :] - 2 * lax.broadcasted_iota(jnp.int32, (lev, cy), 0)
    at_west, at_east = offset == 1, (offset == 2) | (offset == 2 - cy)
    beyond = [
        jnp.sum(jnp.where(at_west, w, 0.0) + jnp.where(at_east, e, 0.0), axis=0, keepdims=True)
        for w, e in corners
    ]
    sub = lax.broadcasted_iota(jnp.int32, (cx, cy), 0)
    above = jnp.where(sub == 0, beyond[0], pltpu.roll(merged, 1, 0))
    below = jnp.where(sub == cx - 1, beyond[1], pltpu.roll(merged, cx - 1, 0))
    less = jnp.where((lane == 1) | (lane == 2), 0.0, pltpu.roll(merged, 2, 1))
    more = jnp.where((lane == cy - 1) | (lane == 0), 0.0, pltpu.roll(merged, cy - 2, 1))
    merged = (
        centre * merged
        + jnp.where(odd, w_gain, e_gain) * (beside + above + below)
        + vert * (less + more)
    )
    ring[2 * lev + cx :, :] = pltpu.roll(jnp.where(odd, merged, pltpu.roll(merged, cy - 2, 1)), cy - 1, 1)


def outer_ring(own, top, bottom, west, east, ngx, ngy):
    cx, cy = west.shape[0] - 8, west.shape[1]
    lev = top.shape[0] // 2 - 4
    return pl.pallas_call(
        functools.partial(ring_kernel, ngx, ngy),
        out_shape=jax.ShapeDtypeStruct((2 * lev + 2 * cx, cy), jnp.float32),
        in_specs=[VMEM] * 5,
        out_specs=VMEM,
        compiler_params=params(8),
        cost_estimate=pl.CostEstimate(flops=10**6, bytes_accessed=10**5, transcendentals=0),
    )(own, top, bottom, west, east)


def step_kernel(ngx, group, second, own, x, *refs):
    if second:
        ring, out, surface, hwet, buf, res, osems = refs
    else:
        top, bottom, res, hwet, buf = refs
    lev, cx, cy = x.shape
    pieces = lev // group

    def leave(i):
        part = pl.ds(i * group, group)
        return pltpu.make_async_copy(res.at[part], out.at[part], osems.at[i])

    ocean = lax.axis_index("mp") == 1
    horiz = jnp.where(ocean, HORIZ[1], HORIZ[0]).astype(jnp.float32)
    vert = jnp.where(ocean, VERT[1], VERT[0]).astype(jnp.float32)
    centre = 1.0 - 4.0 * horiz - 2.0 * vert
    wet = own.at[pl.ds(0, cx)]
    hwet[...] = wet[...] * horiz
    lane = lanes((cx, cy))
    ends = (lane == 0) | (lane == cy - 1)
    height = cx + 2 * PAD
    flat = buf.reshape((lev + 2) * height, cy)
    above, below = pl.ds(height + PAD - 1, lev, stride=height), pl.ds(height + PAD + cx, lev, stride=height)
    if second:
        flat[above, :] = ring[0:lev, :]
        flat[below, :] = ring[lev : 2 * lev, :]
    else:
        gx = lax.axis_index("gx")
        flat[above, :] = top[0:lev, :] * jnp.where(gx > 0, 1.0, 0.0).astype(jnp.float32)
        flat[below, :] = bottom[0:lev, :] * jnp.where(gx < ngx - 1, 1.0, 0.0).astype(jnp.float32)
    buf[0] = jnp.zeros((height, cy), jnp.float32)
    buf[lev + 1] = jnp.zeros((height, cy), jnp.float32)

    apart = lax.broadcasted_iota(jnp.int32, (cy, cy), 0) - lanes((cy, cy))
    pairs = jnp.where((apart == 1) | (apart == -1), 1.0, 0.0).astype(jnp.bfloat16)
    pairs = jnp.concatenate([pairs, pairs], axis=0)

    def beside_of(here):
        high = here.astype(jnp.bfloat16)
        low = (here - high.astype(jnp.float32)).astype(jnp.bfloat16)
        both = jnp.concatenate([high, low], axis=1)
        return jnp.dot(both, pairs, preferred_element_type=jnp.float32)

    def columns(part, start):
        off = 2 * lev + part * cx
        return pltpu.roll(ring[off : off + cx, :], lax.rem(2 * cy - 2 * start, cy), 1)

    def at_ends(sides, j):
        return jnp.where(ends, pltpu.roll(sides, (cy - 2 * j) % cy, 1), 0.0)

    def accept(i):
        sides = columns(0, i * group) if second else None
        for j in range(group):
            here = x[i * group + j]
            here = here + at_ends(sides, j) if second else here * wet[...]
            buf[i * group + j + 1, PAD : PAD + cx, :] = here

    def levels(start, count):
        sides = columns(1, start) if second else None
        for j in range(count):
            l = start + j
            here = buf[l + 1, PAD : PAD + cx, :]
            around = (
                beside_of(here)
                + buf[l + 1, PAD - 1 : PAD - 1 + cx, :]
                + buf[l + 1, PAD + 1 : PAD + 1 + cx, :]
            )
            if second:
                around = around + at_ends(sides, j)
            column = buf[l, PAD : PAD + cx, :] + buf[l + 2, PAD : PAD + cx, :]
            res[l] = centre * here + hwet[...] * around + vert * column

    accept(0)
    levels(0, group - 1)
    if second:
        surface[...] = res[0]

    def middle(i, _):
        accept(i)
        levels(i * group - 1, group)
        if second:
            leave(i - 1).start()
        return 0

    lax.fori_loop(1, pieces, middle, 0)
    levels(lev - 1, 1)
    if second:
        leave(pieces - 1).start()
        for i in range(pieces):
            leave(i).wait()


def one_step(own, x, outside, ngx, second):
    lev, cx, cy = x.shape
    group = 8
    whole = jax.ShapeDtypeStruct(x.shape, jnp.float32)
    return pl.pallas_call(
        functools.partial(step_kernel, ngx, group, second),
        out_shape=(whole, jax.ShapeDtypeStruct((cx, cy), jnp.float32)) if second else whole,
        in_specs=[VMEM] * (2 + len(outside)),
        out_specs=(ANY, VMEM) if second else VMEM,
        scratch_shapes=[
            pltpu.VMEM((cx, cy), jnp.float32),
            pltpu.VMEM((lev + 2, cx + 2 * PAD, cy), jnp.float32),
        ]
        + [pltpu.VMEM(x.shape, jnp.float32), pltpu.SemaphoreType.DMA((lev // group,))] * second,
        compiler_params=params(16),
        cost_estimate=pl.CostEstimate(
            flops=10**6 if second else FIRST_COST, bytes_accessed=10**5, transcendentals=0
        ),
    )(own, x, *outside)


def collect_kernel(ndev, own, got, surface, second, out, received, level, onehot, sums, sems, rsems):
    block = got.shape[0] // ndev
    extra = block - 8 * CAP
    fields, cx, cy = received.shape
    slots = ndev * CAP
    store = pltpu.make_async_copy(level, out.at[0], sems.at[0])

    def leave(i):
        part = pl.ds(i * fields // 2, fields // 2)
        return pltpu.make_async_copy(sums.at[part], received.at[part], rsems.at[i])

    labels = got[block - extra : block, :]
    for s in range(1, ndev):
        labels = labels + got[(s + 1) * block - extra : (s + 1) * block, :]
    labels = labels.astype(jnp.int32)
    want = lax.broadcasted_iota(jnp.int32, (cx, 128), 0) + 1
    wide = jnp.concatenate([labels[q : q + 1, :] == want for q in range(slots // 128)], axis=1)
    hot = jnp.where(wide, 1.0, 0.0).astype(jnp.bfloat16)
    onehot[:, 0:slots] = hot
    onehot[:, slots:] = hot
    for k in range(fields):
        x = jnp.concatenate([got[pl.ds(s * block + k, CAP, stride=8), :] for s in range(ndev)], axis=0)
        high = x.astype(jnp.bfloat16)
        low = (x - high.astype(jnp.float32)).astype(jnp.bfloat16)
        sums[k] = jnp.dot(
            onehot[...], jnp.concatenate([high, low], axis=0), preferred_element_type=jnp.float32
        )
        if k == fields // 2 - 1:
            leave(0).start()
        if k == 0:
            level[...] = surface[...] + FORCE * own[0:cx, :] * sums[0]
            store.start()
    leave(1).start()
    store.wait()
    leave(0).wait()
    leave(1).wait()


def collect(own, got, surface, second, fields, ndev):
    _, cx, cy = second.shape
    return pl.pallas_call(
        functools.partial(collect_kernel, ndev),
        out_shape=(
            jax.ShapeDtypeStruct(second.shape, jnp.float32),
            jax.ShapeDtypeStruct((fields, cx, cy), jnp.float32),
        ),
        in_specs=[VMEM, VMEM, VMEM, ANY],
        out_specs=(ANY, ANY),
        scratch_shapes=[
            pltpu.VMEM((cx, cy), jnp.float32),
            pltpu.VMEM((cx, 2 * ndev * CAP), jnp.bfloat16),
            pltpu.VMEM((fields, cx, cy), jnp.float32),
            pltpu.SemaphoreType.DMA((1,)),
            pltpu.SemaphoreType.DMA((2,)),
        ],
        input_output_aliases={3: 0},
        compiler_params=params(16),
        cost_estimate=pl.CostEstimate(flops=10**8, bytes_accessed=2 * 10**6, transcendentals=0),
    )(own, got, surface, second)


def local(states, surface, land_mask, tile_weights, tile_source, tile_target, tile_row):
    ngx, ngy = lax.axis_size("gx"), lax.axis_size("gy")
    ndev = ngx * ngy
    state, fields = states[0], surface.shape[1]
    cx, cy = land_mask.shape
    ahead = lambda n: [(i, (i + 1) % n) for i in range(n)]
    behind = lambda n: [((i + 1) % n, i) for i in range(n)]
    buckets, up, down, own = outgoing(
        tile_source[0, 0, 0],
        tile_target[0, 0, 0, :, 0],
        tile_row[0, 0, 0],
        land_mask,
        surface.reshape(fields * cx, cy),
        tile_weights[0, 0, 0],
        state,
        ngx,
        ngy,
    )
    top = lax.ppermute(down, "gx", ahead(ngx))
    bottom = lax.ppermute(up, "gx", behind(ngx))
    buckets = lax.ppermute(buckets, "mp", [(0, 1), (1, 0)])
    whole = buckets.shape
    buckets = buckets.reshape(ndev, whole[0] // ndev, 1, whole[1])
    got = lax.all_to_all(buckets, ("gx", "gy"), split_axis=0, concat_axis=0, tiled=True)
    got = got.reshape(whole)
    first, second = relay(own, top, bottom, cx)

    def exchange(x, start):
        other = lambda i: i + 1 if i % 2 == start else i - 1
        return lax.ppermute(x, "gy", [(i, other(i) if 0 <= other(i) < ngy else i) for i in range(ngy)])

    west, east = exchange(first, 0), exchange(second, 1)
    first = one_step(own, state, (top, bottom), ngx, False)
    ring = outer_ring(own, top, bottom, west, east, ngx, ngy)
    second, level = one_step(own, first, (ring,), ngx, True)
    new_state, received = collect(own, got, level, second, fields, ndev)
    return new_state[None], received[None]


def solution(mesh):
    return jax.shard_map(
        local,
        mesh=mesh,
        in_specs=(
            P("mp", None, "gx", "gy"),
            P("mp", None, "gx", "gy"),
            P("gx", "gy"),
            P("mp", "gx", "gy", None, None, None),
            P("mp", "gx", "gy", None),
            P("mp", "gx", "gy", None, None),
            P("mp", "gx", "gy", None),
        ),
        out_specs=(P("mp", None, "gx", "gy"), P("mp", None, "gx", "gy")),
        check_vma=False,
    )
```

```python
import functools

import jax
import jax.numpy as jnp
from jax import lax
from jax.experimental import pallas as pl
from jax.experimental.pallas import tpu as pltpu
from jax.sharding import PartitionSpec as P

CAP = 8
FORCE = 0.5
HORIZ = (0.15, 0.12)
VERT = (0.1, 0.15)
MIB = 1024 * 1024
LIMIT = 60
FIRST_COST = 5 * 10**9
ANY = pl.BlockSpec(memory_space=pl.ANY)
VMEM = pl.BlockSpec(memory_space=pltpu.VMEM)
SMEM = pl.BlockSpec(memory_space=pltpu.SMEM)


def params(mib):
    return pltpu.CompilerParams(vmem_limit_bytes=mib * MIB)


def wet_of(mask_ref):
    ocean = lax.axis_index("mp") == 1
    return jnp.where(ocean, mask_ref[...].astype(jnp.float32), 1.0)


def lanes(shape):
    return lax.broadcasted_iota(jnp.int32, shape, len(shape) - 1)


def parts(lev, cx):
    sizes, start, out = (cx, lev, lev, cx + 8, cx + 8), 0, []
    for size in sizes:
        out.append(pl.ds(start, size))
        start += size
    return out


def send_kernel(
    ndev, ngy, chunk, group, tile_source, tile_target, tile_row, mask, surface, weights, state,
    out, up, down, own,
    src, tgt, row, count, labels, mbuf, sbuf, wbuf, buf, sems, wsems, usems,
):
    lev, cx, cy = state.shape
    tiles, band = weights.shape[0], 64
    wet, up_near, down_near, left, right = (own.at[part] for part in parts(lev, cx))
    held = sbuf.at[pl.ds(0, surface.shape[0])]
    small = [
        pltpu.make_async_copy(a, b, sems.at[i])
        for i, (a, b) in enumerate(
            ((tile_source, src), (tile_target, tgt), (tile_row, row), (mask, mbuf), (surface, held))
        )
    ]
    for copy in small:
        copy.start()
    wcopies, ucopies = [], []
    for i in range(tiles // chunk):
        part = pl.ds(i * chunk, chunk)
        wcopies.append(pltpu.make_async_copy(weights.at[part], wbuf.at[part], wsems.at[i]))
        wcopies[-1].start()
    for i in range(cx // band):
        part = (slice(None), pl.ds(i * band, band), slice(None))
        ucopies.append(pltpu.make_async_copy(state.at[part], buf.at[part], usems.at[i]))
        ucopies[-1].start()
    block = out.shape[0] // ndev
    extra = block - 8 * CAP
    out[...] = jnp.zeros_like(out)
    labels[...] = jnp.zeros_like(labels)
    for d in range(ndev):
        count[d] = 0
    me = lax.axis_index("gx") * ngy + lax.axis_index("gy")
    place = lax.broadcasted_iota(jnp.int32, (8, 128), 0) * 128 + lanes((8, 128))
    for copy in small:
        copy.wait()
    wet[...] = wet_of(mbuf)

    per = 128 // 8
    own_lanes = lanes((cy, 128)) // 8

    def some(start):
        picked = []
        for t in range(start, start + per):
            s = src[t]
            picked.append(sbuf[pl.ds(s, 8, stride=cx), :] * wet[pl.ds(s, 1), :])
        rounded = jnp.concatenate(picked, axis=0).astype(jnp.bfloat16).astype(jnp.float32)
        turned = jnp.transpose(rounded)
        apart = [jnp.where(own_lanes == i, turned, 0.0).astype(jnp.bfloat16) for i in range(per)]
        total = jnp.dot(
            jnp.concatenate([wbuf[start + i] for i in range(per)], axis=1),
            jnp.concatenate(apart, axis=0),
            preferred_element_type=jnp.float32,
        )
        total = jnp.transpose(total)
        for i in range(per):
            t = start + i
            d = tgt[t]
            rank = count[d]
            count[d] = rank + 1
            out[pl.ds(d * block + rank * 8, 8), :] = total[i * 8 : (i + 1) * 8, :]
            label = (row[t] + 1).astype(jnp.float32)
            labels[d] = jnp.where(place == me * CAP + rank, label, labels[d])

    for i in range(tiles // chunk):
        wcopies[i].wait()
        for start in range(i * chunk, (i + 1) * chunk, per):
            some(start)
    for d in range(ndev):
        out[(d + 1) * block - extra : (d + 1) * block, :] = labels[d, 0:extra, :]

    turned = jnp.transpose(wet[...])
    up[2 * lev :, :] = jnp.broadcast_to(wet[0:1, :], (8, cy))
    down[2 * lev :, :] = jnp.broadcast_to(wet[cx - 1 :, :], (8, cy))
    left[cx:, :] = jnp.broadcast_to(turned[0:1, :], (8, cx))
    right[cx:, :] = jnp.broadcast_to(turned[cy - 1 :, :], (8, cx))
    strip = 32
    flat = buf.reshape(lev * cx, cy)
    lane = lanes((strip, cy))
    even, low_half = lane % 2 == 0, lane % 4 < 2
    fours = lane // 4, lax.rem(lane + cy - 2, cy) // 4
    for i in range(cx // band):
        ucopies[i].wait()
        for b in range(i * band // strip, (i + 1) * band // strip):
            rows = pl.ds(b * strip, strip)
            gathered = [jnp.zeros((strip, cy), jnp.float32)] * 2
            for l in range(lev):
                moved = pltpu.roll(buf[l, rows, :], (2 * l + 2) % cy, 1)
                gathered[l % 2] = jnp.where(fours[l % 2] == l // 2, moved, gathered[l % 2])
            edge = wet[rows, :]
            lo = jnp.where(low_half, gathered[1], gathered[0])
            hi = jnp.where(low_half, gathered[0], gathered[1])
            left[rows, :] = lo * jnp.where(even, edge[:, 0:1], edge[:, 1:2])
            right[rows, :] = hi * jnp.where(even, edge[:, cy - 2 : cy - 1], edge[:, cy - 1 :])
    for dst, off, r in ((up, 0, 0), (up, lev, 1), (down, 0, cx - 1), (down, lev, cx - 2)):
        dst[off : off + lev, :] = flat[pl.ds(r, lev, stride=cx), :] * wet[r : r + 1, :]
    up_near[...] = up[0:lev, :]
    down_near[...] = down[0:lev, :]


def outgoing(tile_source, tile_target, tile_row, mask, surface, weights, state, ngx, ngy):
    tiles = weights.shape[0]
    lev, cx, cy = state.shape
    ndev, chunk, group = ngx * ngy, 32, lev
    block = 8 * CAP + ndev * CAP // 128
    message = jax.ShapeDtypeStruct((2 * lev + 8, cy), jnp.float32)
    return pl.pallas_call(
        functools.partial(send_kernel, ndev, ngy, chunk, group),
        out_shape=(
            jax.ShapeDtypeStruct((ndev * block, 128), jnp.float32),
            message,
            message,
            jax.ShapeDtypeStruct((parts(lev, cx)[-1].start + cx + 8, cy), jnp.float32),
        ),
        in_specs=[ANY] * 7,
        out_specs=(VMEM,) * 4,
        scratch_shapes=[
            pltpu.SMEM((tiles,), jnp.int32),
            pltpu.SMEM((tiles,), jnp.int32),
            pltpu.SMEM((tiles,), jnp.int32),
            pltpu.SMEM((ndev,), jnp.int32),
            pltpu.VMEM((ndev, 8, 128), jnp.float32),
            pltpu.VMEM(mask.shape, jnp.int32),
            pltpu.VMEM((surface.shape[0] + cx, cy), jnp.float32),
            pltpu.VMEM(weights.shape, weights.dtype),
            pltpu.VMEM(state.shape, jnp.float32),
            pltpu.SemaphoreType.DMA((5,)),
            pltpu.SemaphoreType.DMA((tiles // chunk,)),
            pltpu.SemaphoreType.DMA((4,)),
        ],
        compiler_params=params(16),
        cost_estimate=pl.CostEstimate(flops=10**8, bytes_accessed=8 * 10**6, transcendentals=0),
    )(
        *[
            pltpu.with_memory_space_constraint(x, pltpu.HBM)
            for x in (tile_source, tile_target, tile_row, mask, surface, weights, state)
        ]
    )


def shifted(x, by, axis):
    size = x.shape[axis]
    moved = pltpu.roll(x, by % size, axis)
    index = lax.broadcasted_iota(jnp.int32, x.shape, axis)
    return jnp.where(index == (0 if by == 1 else size - 1), 0.0, moved)


PAD = 8


def relay_kernel(own, top, bottom, first, second):
    cx = first.shape[0] - 8
    cy = first.shape[1]
    lev = top.shape[0] // 2 - 4
    eye = lanes((lev, cy)) == lax.broadcasted_iota(jnp.int32, (lev, cy), 0)
    even = lax.rem(lax.axis_index("gy"), 2) == 0
    west, east = (own[part, :] for part in parts(lev, cx)[3:])
    first[...] = jnp.where(even, east, west)
    second[...] = jnp.where(even, west, east)
    for out, turn in ((first, even), (second, jnp.logical_not(even))):
        for i, msg in enumerate((top, bottom)):
            column = jnp.where(turn, msg[0:lev, cy - 1 : cy], msg[0:lev, 0:1])
            row = jnp.sum(jnp.where(eye, column, 0.0), axis=0, keepdims=True)
            out[cx + 1 + i : cx + 2 + i, :] = row


def relay(own, top, bottom, cx):
    cy = own.shape[1]
    columns = jax.ShapeDtypeStruct((cx + 8, cy), jnp.float32)
    return pl.pallas_call(
        relay_kernel,
        out_shape=(columns, columns),
        in_specs=[VMEM] * 3,
        out_specs=(VMEM, VMEM),
        compiler_params=params(8),
        cost_estimate=pl.CostEstimate(flops=10**11, bytes_accessed=10**8, transcendentals=0),
    )(own, top, bottom)


def ring_kernel(ngx, ngy, own, top, bottom, got_a, got_b, ring):
    cx, cy = got_a.shape[0] - 8, got_a.shape[1]
    even = lax.rem(lax.axis_index("gy"), 2) == 0
    a, b = got_a[...], got_b[...]
    west, east = jnp.where(even, b, a), jnp.where(even, a, b)
    lev = top.shape[0] // 2 - 4
    wet, up, down, left, right = (own.at[part] for part in parts(lev, cx))
    ocean = lax.axis_index("mp") == 1
    horiz = jnp.where(ocean, HORIZ[1], HORIZ[0]).astype(jnp.float32)
    vert = jnp.where(ocean, VERT[1], VERT[0]).astype(jnp.float32)
    centre = 1.0 - 4.0 * horiz - 2.0 * vert
    gx, gy = lax.axis_index("gx"), lax.axis_index("gy")
    has = lambda c: jnp.where(c, 1.0, 0.0).astype(jnp.float32)
    has_top, has_bottom = has(gx > 0), has(gx < ngx - 1)
    has_west, has_east = has(gy > 0), has(gy < ngy - 1)

    lane = lanes((lev, cy))
    eye = lane == lax.broadcasted_iota(jnp.int32, (lev, cy), 0)

    def corner(msg, i, flag):
        row = msg[cx + 1 + i : cx + 2 + i, :]
        return flag * jnp.sum(jnp.where(eye, row, 0.0), axis=1, keepdims=True)

    corners = [
        (corner(west, i, flag * has_west), corner(east, i, flag * has_east))
        for i, flag in enumerate((has_top, has_bottom))
    ]
    for msg, mine, flag, i in ((top, up, has_top, 0), (bottom, down, has_bottom, 1)):
        near = msg[0:lev, :] * flag
        far = msg[lev : 2 * lev, :] * flag
        w_corner, e_corner = corners[i]
        side = pltpu.roll(jnp.where(lane == cy - 1, w_corner, near), 1, 1) + pltpu.roll(
            jnp.where(lane == 0, e_corner, near), cy - 1, 1
        )
        gain = msg[2 * lev : 2 * lev + 1, :] * (horiz * flag)
        outer = (
            centre * near
            + gain * (side + far + mine[...])
            + vert * (shifted(near, 1, 0) + shifted(near, -1, 0))
        )
        ring[i * lev : (i + 1) * lev, :] = outer

    lane = lanes((cx, cy))
    odd = lane % 2 == 1
    west_cols = west[0:cx, :] * has_west
    east_cols = east[0:cx, :] * has_east
    w_gain = jnp.transpose(jnp.broadcast_to(west[cx : cx + 1, :], (cx, cx))) * (horiz * has_west)
    e_gain = jnp.transpose(jnp.broadcast_to(east[cx : cx + 1, :], (cx, cx))) * (horiz * has_east)
    merged = jnp.where(odd, west_cols, east_cols)
    given = merged * (horiz * jnp.where(odd, wet[:, 0:1], wet[:, cy - 1 : cy]))
    ring[2 * lev : 2 * lev + cx, :] = pltpu.roll(
        jnp.where(odd, given, pltpu.roll(given, cy - 2, 1)), cy - 1, 1
    )
    beside = (
        jnp.where(odd, pltpu.roll(west_cols, 1, 1), pltpu.roll(east_cols, cy - 1, 1))
        + jnp.where(odd, pltpu.roll(left[0:cx, :], cy - 1, 1), pltpu.roll(right[0:cx, :], 1, 1))
    )
    offset = lane[0:lev, :] - 2 * lax.broadcasted_iota(jnp.int32, (lev, cy), 0)
    at_west, at_east = offset == 1, (offset == 2) | (offset == 2 - cy)
    beyond = [
        jnp.sum(jnp.where(at_west, w, 0.0) + jnp.where(at_east, e, 0.0), axis=0, keepdims=True)
        for w, e in corners
    ]
    sub = lax.broadcasted_iota(jnp.int32, (cx, cy), 0)
    above = jnp.where(sub == 0, beyond[0], pltpu.roll(merged, 1, 0))
    below = jnp.where(sub == cx - 1, beyond[1], pltpu.roll(merged, cx - 1, 0))
    less = jnp.where((lane == 1) | (lane == 2), 0.0, pltpu.roll(merged, 2, 1))
    more = jnp.where((lane == cy - 1) | (lane == 0), 0.0, pltpu.roll(merged, cy - 2, 1))
    merged = (
        centre * merged
        + jnp.where(odd, w_gain, e_gain) * (beside + above + below)
        + vert * (less + more)
    )
    ring[2 * lev + cx :, :] = pltpu.roll(jnp.where(odd, merged, pltpu.roll(merged, cy - 2, 1)), cy - 1, 1)


def outer_ring(own, top, bottom, west, east, ngx, ngy):
    cx, cy = west.shape[0] - 8, west.shape[1]
    lev = top.shape[0] // 2 - 4
    return pl.pallas_call(
        functools.partial(ring_kernel, ngx, ngy),
        out_shape=jax.ShapeDtypeStruct((2 * lev + 2 * cx, cy), jnp.float32),
        in_specs=[VMEM] * 5,
        out_specs=VMEM,
        compiler_params=params(8),
        cost_estimate=pl.CostEstimate(flops=10**6, bytes_accessed=10**5, transcendentals=0),
    )(own, top, bottom, west, east)


def step_kernel(ngx, group, second, own, x, *refs):
    if second:
        ring, out, surface, hwet, buf, res, osems = refs
    else:
        top, bottom, res, hwet, buf = refs
    lev, cx, cy = x.shape
    pieces = lev // group

    def leave(i):
        part = pl.ds(i * group, group)
        return pltpu.make_async_copy(res.at[part], out.at[part], osems.at[i])

    ocean = lax.axis_index("mp") == 1
    horiz = jnp.where(ocean, HORIZ[1], HORIZ[0]).astype(jnp.float32)
    vert = jnp.where(ocean, VERT[1], VERT[0]).astype(jnp.float32)
    centre = 1.0 - 4.0 * horiz - 2.0 * vert
    wet = own.at[pl.ds(0, cx)]
    hwet[...] = wet[...] * horiz
    lane = lanes((cx, cy))
    ends = (lane == 0) | (lane == cy - 1)
    height = cx + 2 * PAD
    flat = buf.reshape((lev + 2) * height, cy)
    above, below = pl.ds(height + PAD - 1, lev, stride=height), pl.ds(height + PAD + cx, lev, stride=height)
    if second:
        flat[above, :] = ring[0:lev, :]
        flat[below, :] = ring[lev : 2 * lev, :]
    else:
        gx = lax.axis_index("gx")
        flat[above, :] = top[0:lev, :] * jnp.where(gx > 0, 1.0, 0.0).astype(jnp.float32)
        flat[below, :] = bottom[0:lev, :] * jnp.where(gx < ngx - 1, 1.0, 0.0).astype(jnp.float32)
    buf[0] = jnp.zeros((height, cy), jnp.float32)
    buf[lev + 1] = jnp.zeros((height, cy), jnp.float32)

    apart = lax.broadcasted_iota(jnp.int32, (cy, cy), 0) - lanes((cy, cy))
    pairs = jnp.where((apart == 1) | (apart == -1), 1.0, 0.0).astype(jnp.bfloat16)
    pairs = jnp.concatenate([pairs, pairs], axis=0)

    def beside_of(here):
        high = here.astype(jnp.bfloat16)
        low = (here - high.astype(jnp.float32)).astype(jnp.bfloat16)
        both = jnp.concatenate([high, low], axis=1)
        return jnp.dot(both, pairs, preferred_element_type=jnp.float32)

    def columns(part, start):
        off = 2 * lev + part * cx
        return pltpu.roll(ring[off : off + cx, :], lax.rem(2 * cy - 2 * start, cy), 1)

    def at_ends(sides, j):
        return jnp.where(ends, pltpu.roll(sides, (cy - 2 * j) % cy, 1), 0.0)

    def accept(i):
        sides = columns(0, i * group) if second else None
        for j in range(group):
            here = x[i * group + j]
            here = here + at_ends(sides, j) if second else here * wet[...]
            buf[i * group + j + 1, PAD : PAD + cx, :] = here

    def levels(start, count):
        sides = columns(1, start) if second else None
        for j in range(count):
            l = start + j
            here = buf[l + 1, PAD : PAD + cx, :]
            around = (
                beside_of(here)
                + buf[l + 1, PAD - 1 : PAD - 1 + cx, :]
                + buf[l + 1, PAD + 1 : PAD + 1 + cx, :]
            )
            if second:
                around = around + at_ends(sides, j)
            column = buf[l, PAD : PAD + cx, :] + buf[l + 2, PAD : PAD + cx, :]
            res[l] = centre * here + hwet[...] * around + vert * column

    accept(0)
    levels(0, group - 1)
    if second:
        surface[...] = res[0]

    def middle(i, _):
        accept(i)
        levels(i * group - 1, group)
        if second:
            leave(i - 1).start()
        return 0

    lax.fori_loop(1, pieces, middle, 0)
    levels(lev - 1, 1)
    if second:
        leave(pieces - 1).start()
        for i in range(pieces):
            leave(i).wait()


def one_step(own, x, outside, ngx, second):
    lev, cx, cy = x.shape
    group = 8
    whole = jax.ShapeDtypeStruct(x.shape, jnp.float32)
    return pl.pallas_call(
        functools.partial(step_kernel, ngx, group, second),
        out_shape=(whole, jax.ShapeDtypeStruct((cx, cy), jnp.float32)) if second else whole,
        in_specs=[VMEM] * (2 + len(outside)),
        out_specs=(ANY, VMEM) if second else VMEM,
        scratch_shapes=[
            pltpu.VMEM((cx, cy), jnp.float32),
            pltpu.VMEM((lev + 2, cx + 2 * PAD, cy), jnp.float32),
        ]
        + [pltpu.VMEM(x.shape, jnp.float32), pltpu.SemaphoreType.DMA((lev // group,))] * second,
        compiler_params=params(16),
        cost_estimate=pl.CostEstimate(
            flops=10**6 if second else FIRST_COST, bytes_accessed=10**5, transcendentals=0
        ),
    )(own, x, *outside)


def collect_kernel(ndev, own, got, surface, second, out, received, level, onehot, sums, sems, rsems):
    block = got.shape[0] // ndev
    extra = block - 8 * CAP
    fields, cx, cy = received.shape
    slots = ndev * CAP
    store = pltpu.make_async_copy(level, out.at[0], sems.at[0])

    def leave(i):
        part = pl.ds(i * (fields - 2), (fields - 2, 2)[i])
        return pltpu.make_async_copy(sums.at[part], received.at[part], rsems.at[i])

    labels = got[block - extra : block, :]
    for s in range(1, ndev):
        labels = labels + got[(s + 1) * block - extra : (s + 1) * block, :]
    labels = labels.astype(jnp.int32)
    want = lax.broadcasted_iota(jnp.int32, (cx, 128), 0) + 1
    wide = jnp.concatenate([labels[q : q + 1, :] == want for q in range(slots // 128)], axis=1)
    hot = jnp.where(wide, 1.0, 0.0).astype(jnp.bfloat16)
    onehot[:, 0:slots] = hot
    onehot[:, slots:] = hot
    for k in range(fields):
        x = jnp.concatenate([got[pl.ds(s * block + k, CAP, stride=8), :] for s in range(ndev)], axis=0)
        high = x.astype(jnp.bfloat16)
        low = (x - high.astype(jnp.float32)).astype(jnp.bfloat16)
        sums[k] = jnp.dot(
            onehot[...], jnp.concatenate([high, low], axis=0), preferred_element_type=jnp.float32
        )
        if k == fields - 3:
            leave(0).start()
        if k == 0:
            level[...] = surface[...] + FORCE * own[0:cx, :] * sums[0]
            store.start()
    leave(1).start()
    store.wait()
    leave(0).wait()
    leave(1).wait()


def collect(own, got, surface, second, fields, ndev):
    _, cx, cy = second.shape
    return pl.pallas_call(
        functools.partial(collect_kernel, ndev),
        out_shape=(
            jax.ShapeDtypeStruct(second.shape, jnp.float32),
            jax.ShapeDtypeStruct((fields, cx, cy), jnp.float32),
        ),
        in_specs=[VMEM, VMEM, VMEM, ANY],
        out_specs=(ANY, ANY),
        scratch_shapes=[
            pltpu.VMEM((cx, cy), jnp.float32),
            pltpu.VMEM((cx, 2 * ndev * CAP), jnp.bfloat16),
            pltpu.VMEM((fields, cx, cy), jnp.float32),
            pltpu.SemaphoreType.DMA((1,)),
            pltpu.SemaphoreType.DMA((2,)),
        ],
        input_output_aliases={3: 0},
        compiler_params=params(16),
        cost_estimate=pl.CostEstimate(flops=10**8, bytes_accessed=2 * 10**6, transcendentals=0),
    )(own, got, surface, second)


def local(states, surface, land_mask, tile_weights, tile_source, tile_target, tile_row):
    ngx, ngy = lax.axis_size("gx"), lax.axis_size("gy")
    ndev = ngx * ngy
    state, fields = states[0], surface.shape[1]
    cx, cy = land_mask.shape
    ahead = lambda n: [(i, (i + 1) % n) for i in range(n)]
    behind = lambda n: [((i + 1) % n, i) for i in range(n)]
    buckets, up, down, own = outgoing(
        tile_source[0, 0, 0],
        tile_target[0, 0, 0, :, 0],
        tile_row[0, 0, 0],
        land_mask,
        surface.reshape(fields * cx, cy),
        tile_weights[0, 0, 0],
        state,
        ngx,
        ngy,
    )
    top = lax.ppermute(down, "gx", ahead(ngx))
    bottom = lax.ppermute(up, "gx", behind(ngx))
    buckets = lax.ppermute(buckets, "mp", [(0, 1), (1, 0)])
    whole = buckets.shape
    buckets = buckets.reshape(ndev, whole[0] // ndev, 1, whole[1])
    got = lax.all_to_all(buckets, ("gx", "gy"), split_axis=0, concat_axis=0, tiled=True)
    got = got.reshape(whole)
    first, second = relay(own, top, bottom, cx)

    def exchange(x, start):
        other = lambda i: i + 1 if i % 2 == start else i - 1
        return lax.ppermute(x, "gy", [(i, other(i) if 0 <= other(i) < ngy else i) for i in range(ngy)])

    east = exchange(second, 1)
    west = exchange(first, 0)
    first = one_step(own, state, (top, bottom), ngx, False)
    ring = outer_ring(own, top, bottom, west, east, ngx, ngy)
    second, level = one_step(own, first, (ring,), ngx, True)
    new_state, received = collect(own, got, level, second, fields, ndev)
    return new_state[None], received[None]


def solution(mesh):
    return jax.shard_map(
        local,
        mesh=mesh,
        in_specs=(
            P("mp", None, "gx", "gy"),
            P("mp", None, "gx", "gy"),
            P("gx", "gy"),
            P("mp", "gx", "gy", None, None, None),
            P("mp", "gx", "gy", None),
            P("mp", "gx", "gy", None, None),
            P("mp", "gx", "gy", None),
        ),
        out_specs=(P("mp", None, "gx", "gy"), P("mp", None, "gx", "gy")),
        check_vma=False,
    )
```
